32 devices in a mesh: groups: 2 (over x), track: 4 (over y, core), frame: 4 (over z).
Axes of the slice: x: 2, y: 2, z: 4, core: 2. Of those that a mesh axis runs over, the one named last changes fastest.
Arguments:
- frames: bfloat16 [16, 4096, 256], P(('groups', 'frame')), parts along dimension 0, may hold values from -9 to 9
- query_frame: int32 [1024], P(('groups', 'track')), parts along dimension 0, may hold values from 0 to 7
- query_pixel: int32 [1024], P(('groups', 'track')), parts along dimension 0, may hold values from 0 to 4095
- cotangent: float32 [2, 16, 512], P(None, ('groups', 'frame'), 'track'), parts along dimension 1, may hold values from -48 to 48
Outputs:
- frame_grad: float32 [4096, 16, 256], P('track', ('groups', 'frame')), parts along dimension 1
- query_grad: float32 [1024, 256], P(('groups', 'track', 'frame')), parts along dimension 0
The draws below stay inside these ranges and needn't reach their ends.
There are 2 independent parts, one for each index of `groups`. The reference program is written for one: setup_inputs(seed, part) draws one part's arguments, and reference() takes and returns one part's arrays. A program takes and returns all parts, laid end to end along the dimension named above; each array names one. Nothing has to cross between parts.
All inputs are finite; a program needn't handle non-finite values.
Results may differ from the reference program's by a relative error of at most 0.0029.
Values may be sent and summed in bfloat16 or wider, within the bound.
A program may use at most 64 MiB of HBM per device.

```python
import jax
import jax.numpy as jnp
from jax import lax

C = 256
FEAT_H = 64
FEAT_W = 64
PIXELS = 4096
FRAMES = 8
TRACKS = 512


def draw_frames(key, part):
    subkeys = jax.random.split(key, 1)
    values = jnp.clip(jax.random.normal(subkeys[0], (FRAMES, PIXELS, C), jnp.float32), -4.5, 4.5)
    return values.astype(jnp.bfloat16)


def plant(result, rng, low, high):
    spot = [jax.random.randint(jax.random.fold_in(rng, axis), (), 0, length) for axis, length in enumerate(result.shape)]
    main_axis = result.shape.index(max(result.shape))
    beside = spot[:main_axis] + [(spot[main_axis] + 1) % result.shape[main_axis]] + spot[main_axis + 1:]
    return result.at[tuple(spot)].set(low).at[tuple(beside)].set(high)


def block_scale(stream_key, shape, cuts, low, largest):
    def one(axis_at, parts):
        draws = jax.random.uniform(jax.random.fold_in(jax.random.fold_in(stream_key, 6), axis_at), (parts,), jnp.float32, low / len(cuts), largest / len(cuts))
        return jnp.repeat(jnp.exp(draws), shape[axis_at] // parts).reshape((-1,) + (1,) * (len(shape) - axis_at - 1))

    level = one(*cuts[0])
    for cut in cuts[1:]:
        level = level * one(*cut)
    return level


def bell_draw(own_key, shape, width, bound, shards=(), dtype=jnp.bfloat16):
    values = jax.random.normal(own_key, shape, jnp.float32) * width
    if len(shards) > 0:
        values = block_scale(own_key, shape, shards, -0.22, 0.18) * values
    return jnp.clip(values, min=-bound, max=bound).astype(dtype)


def setup_inputs(seed: int = 0, part: int = 0) -> dict:
    seeds = jax.random.split(jax.random.key(seed), 5)
    part_keys = jax.random.split(jax.random.fold_in(seeds[4], part), 5)
    return {
        "frames": draw_frames(jax.random.fold_in(jax.random.fold_in(seeds[4], part), 71), part),
        "query_frame": plant(jax.random.randint(part_keys[1], (TRACKS,), 0, FRAMES), jax.random.fold_in(part_keys[1], 1), 0, FRAMES - 1).astype(jnp.int32),
        "query_pixel": plant(jax.random.randint(part_keys[2], (TRACKS,), 0, PIXELS), jax.random.fold_in(part_keys[2], 1), 0, PIXELS - 1).astype(jnp.int32),
        "cotangent": bell_draw(part_keys[3], (2, FRAMES, TRACKS), 8.0, 48.0, ((1, 4), (2, 4)), jnp.float32),
    }


def reference(frames, query_frame, query_pixel, cotangent):
    all_pixels = frames.reshape(FRAMES * PIXELS, C)
    row_index = (query_frame * PIXELS + query_pixel).astype(jnp.int32)
    query_feat = all_pixels[row_index]
    score_scale = C ** -0.5
    pixel_ids = jnp.arange(PIXELS)
    coord_x = ((pixel_ids % FEAT_W) * (2.0 / (FEAT_W - 1)) - 1.0).astype(jnp.float32)
    coord_y = ((pixel_ids // FEAT_W) * (2.0 / (FEAT_H - 1)) - 1.0).astype(jnp.float32)

    def per_frame(total_grad, inputs):
        one_frame, frame_cot = inputs
        scores = jnp.dot(query_feat, one_frame.T, preferred_element_type=jnp.float32) * score_scale
        peak_score = jnp.max(scores, axis=1, keepdims=True)
        exp_scores = jnp.exp(scores - peak_score)
        weights = exp_scores / jnp.sum(exp_scores, axis=1, keepdims=True)
        expect_x = jnp.sum(weights * coord_x[None, :], axis=1)
        expect_y = jnp.sum(weights * coord_y[None, :], axis=1)
        grad_x = frame_cot[0]
        grad_y = frame_cot[1]
        inner_sum = grad_x * expect_x + grad_y * expect_y
        cost_grad = (weights * (grad_x[:, None] * coord_x[None, :] + grad_y[:, None] * coord_y[None, :] - inner_sum[:, None]) * score_scale).astype(jnp.bfloat16)
        image_grad = jnp.dot(cost_grad.T, query_feat, preferred_element_type=jnp.float32)
        total_grad = total_grad + jnp.dot(cost_grad, one_frame, preferred_element_type=jnp.float32)
        return total_grad, image_grad

    query_grad, frame_grads = lax.scan(per_frame, jnp.zeros((TRACKS, C), jnp.float32), (frames, jnp.moveaxis(cotangent, 1, 0)))
    frame_grad = jnp.transpose(frame_grads, (1, 0, 2))
    return frame_grad, query_grad
```

```python
import functools
import math

import jax
import jax.numpy as jnp
from jax import lax
from jax.experimental import pallas as pl
from jax.experimental.pallas import tpu as pltpu
from jax.sharding import PartitionSpec as P

C = 256
FEAT_H = 64
FEAT_W = 64
LANES = 128
MESH = pl.DeviceIdType.MESH
SCORE_SCALE = C ** (-0.5)
LOG2_SCALE = SCORE_SCALE * math.log2(math.e)
STEP_X = 2.0 / (FEAT_W - 1)
STEP_Y = 2.0 / (FEAT_H - 1)


def dot(a, b, dims):
    return lax.dot_general(a, b, (dims, ((), ())), preferred_element_type=jnp.float32)


def kernel(
    n_track,
    n_frame,
    frames_hbm,
    query_frame_ref,
    query_pixel_ref,
    cot_ref,
    out_ref,
    query_out_ref,
    fr,
    scores,
    picked,
    picked_in,
    feats,
    stats,
    term,
    term_in,
    load_sem,
    pick_send,
    pick_recv,
    ring_send,
    ring_recv,
    feat_send,
    feat_recv,
    stat_send,
    stat_recv,
    term_send,
    term_recv,
):
    held, pixels, channels = fr.shape
    q = cot_ref.shape[2]
    rows = q // n_frame
    block = pixels // n_track
    me_t = lax.axis_index("track")
    me_f = lax.axis_index("frame")

    def peers(name, me, n):
        return [(d, {name: lax.rem(me + d, n)}) for d in range(1, n)]

    track_peers = peers("track", me_t, n_track)
    frame_peers = peers("frame", me_f, n_frame)

    barrier = pltpu.get_barrier_semaphore()
    for _, device in track_peers + frame_peers:
        pl.semaphore_signal(barrier, inc=1, device_id=device, device_id_type=MESH)

    parts = load_sem.shape[1]
    piece = pixels // parts
    loads = []
    for t in range(held):
        for i in range(parts):
            where = pl.ds(i * piece, piece)
            load = pltpu.make_async_copy(frames_hbm.at[t, where], fr.at[t, where], load_sem.at[t, i])
            load.start()
            loads.append((t, i, load))

    eye = lax.broadcasted_iota(jnp.int32, (q, q), 0) == lax.broadcasted_iota(jnp.int32, (q, q), 1)

    def to_column(row):
        return jnp.sum(jnp.where(eye, row, jnp.zeros_like(row)), axis=1, keepdims=True)

    def to_row(column):
        return jnp.sum(jnp.where(eye, column, jnp.zeros_like(column)), axis=0, keepdims=True)

    index = (query_frame_ref[...] - me_f * held) * pixels + query_pixel_ref[...]
    index = to_column(index.astype(jnp.float32)).astype(jnp.int32)
    lane = lax.broadcasted_iota(jnp.int32, (q, piece), 1)
    total = jnp.zeros((q, channels), jnp.float32)
    for t, i, load in loads:
        load.wait()
        hot = jnp.where(lane == index - (t * pixels + i * piece), 1.0, 0.0).astype(jnp.bfloat16)
        total += dot(hot, fr[t, i * piece : (i + 1) * piece, :], ((1,), (0,)))
    picked[...] = total.astype(jnp.bfloat16).reshape(n_frame, rows, channels)

    pl.semaphore_wait(barrier, n_track + n_frame - 2)

    copies = []
    for d, device in frame_peers:
        copies.append(
            pltpu.make_async_remote_copy(
                src_ref=picked.at[lax.rem(me_f + d, n_frame)],
                dst_ref=picked_in.at[d],
                send_sem=pick_send.at[d],
                recv_sem=pick_recv.at[d],
                device_id=device,
                device_id_type=MESH,
            )
        )
        copies[-1].start()
    mine = picked[me_f].astype(jnp.float32)
    for d, copy in enumerate(copies, 1):
        copy.wait_recv()
        mine += picked_in[d].astype(jnp.float32)
    feats[me_t, me_f] = mine.astype(jnp.bfloat16)
    sends = copies
    copies = []
    for d, device in frame_peers:
        copies.append(
            pltpu.make_async_remote_copy(
                src_ref=feats.at[me_t, me_f],
                dst_ref=feats.at[me_t, me_f],
                send_sem=ring_send.at[d],
                recv_sem=ring_recv.at[d],
                device_id=device,
                device_id_type=MESH,
            )
        )
        copies[-1].start()
    for copy in copies:
        copy.wait_recv()
    sends += copies
    feat_copies = []
    for d, device in track_peers:
        feat_copies.append(
            pltpu.make_async_remote_copy(
                src_ref=feats.at[me_t],
                dst_ref=feats.at[me_t],
                send_sem=feat_send.at[d],
                recv_sem=feat_recv.at[d],
                device_id=device,
                device_id_type=MESH,
            )
        )
        feat_copies[-1].start()
    sends += feat_copies

    own = feats[me_t].reshape(q, channels)
    wide = scores.shape[3]
    cols = wide // LANES
    chunks = pixels // wide
    lane = lax.broadcasted_iota(jnp.int32, (q, LANES), 1)
    lane_x = (lane % FEAT_W).astype(jnp.float32)
    lane_y = (lane // FEAT_W).astype(jnp.float32)
    row_step = LANES // FEAT_W

    def split(x):
        return [x[:, c * LANES : (c + 1) * LANES] for c in range(cols)]

    def chunk_of(t, i):
        return fr[t, pl.ds(pl.multiple_of(i * wide, wide), wide), :]

    peaks = []
    for t in range(held):

        def score(i, peak):
            s = dot(own, chunk_of(t, i), ((1,), (1,)))
            scores[t, i] = s
            return functools.reduce(jnp.maximum, split(s), peak)

        peak = lax.fori_loop(0, chunks, score, jnp.full((q, LANES), -jnp.inf, jnp.float32))
        peaks.append(jnp.max(peak, axis=1, keepdims=True) * LOG2_SCALE)

    columns = []
    for t in range(held):

        def expo(i, carry):
            zero, first = carry
            e = jnp.exp2(scores[t, i] * LOG2_SCALE - peaks[t])
            scores[t, i] = e
            e = split(e)
            tail = e[-1]
            moment = tail
            for part in e[-2:0:-1]:
                tail = tail + part
                moment = moment + tail
            tail = tail + e[0]
            return zero + tail, first + (moment + tail * (i * cols).astype(jnp.float32))

        empty = jnp.zeros((q, LANES), jnp.float32)
        zero, first = lax.fori_loop(0, chunks, expo, (empty, empty))
        mass = jnp.sum(zero, axis=1, keepdims=True)
        mean_x = jnp.sum(zero * lane_x, axis=1, keepdims=True) / mass
        mean_y = jnp.sum(zero * lane_y + first * row_step, axis=1, keepdims=True) / mass
        grad_x = to_column(cot_ref[0, t : t + 1, :])
        grad_y = to_column(cot_ref[1, t : t + 1, :])
        scale = SCORE_SCALE / mass
        slope_x = grad_x * STEP_X * scale
        slope_y = grad_y * STEP_Y * scale
        columns.append((slope_x, slope_y, -(slope_x * mean_x + slope_y * mean_y)))

    for t in range(held):
        for i, column in enumerate((peaks[t],) + columns[t]):
            stats[me_t, 4 * t + i : 4 * t + i + 1, :] = to_row(column)
    stat_copies = []
    for d, device in track_peers:
        stat_copies.append(
            pltpu.make_async_remote_copy(
                src_ref=stats.at[me_t],
                dst_ref=stats.at[me_t],
                send_sem=stat_send.at[d],
                recv_sem=stat_recv.at[d],
                device_id=device,
                device_id_type=MESH,
            )
        )
        stat_copies[-1].start()
    sends += stat_copies

    total = jnp.zeros((q, channels), jnp.float32)
    for t in range(held):
        slope_x, slope_y, level = columns[t]
        base = level + slope_x * lane_x + slope_y * lane_y
        step = slope_y * row_step

        def query_part(i, total):
            at = [base + step * (i * cols + c).astype(jnp.float32) for c in range(cols)]
            grad = (scores[t, i] * jnp.concatenate(at, axis=1)).astype(jnp.bfloat16)
            return total + dot(grad, chunk_of(t, i), ((1,), (0,)))

        total = lax.fori_loop(0, chunks, query_part, total)
    term[...] = total.reshape(n_frame, rows, channels)
    term_copies = []
    for d, device in frame_peers:
        term_copies.append(
            pltpu.make_async_remote_copy(
                src_ref=term.at[lax.rem(me_f + d, n_frame)],
                dst_ref=term_in.at[d],
                send_sem=term_send.at[d],
                recv_sem=term_recv.at[d],
                device_id=device,
                device_id_type=MESH,
            )
        )
        term_copies[-1].start()
    sends += term_copies

    for copy in feat_copies + stat_copies:
        copy.wait_recv()
    tracks = n_track * q
    everyone = feats[...].reshape(tracks, channels)
    levels = jnp.concatenate([stats[k] for k in range(n_track)], axis=1)
    size = max(FEAT_W, min(block, 131072 // tracks // FEAT_W * FEAT_W))
    lines = size // FEAT_W
    tiles = channels // LANES
    column_x = lax.broadcasted_iota(jnp.int32, (FEAT_W, 1), 0).astype(jnp.float32)
    slopes = [levels[4 * t + 1 : 4 * t + 2] * column_x for t in range(held)]

    def frame_part(i, carry):
        start = me_t * block + i * size
        first_line = me_t * (block // FEAT_W) + i * lines
        for t in range(held):
            peak, _, slope_y, level = [levels[4 * t + j : 4 * t + j + 1] for j in range(4)]
            s = dot(fr[t, pl.ds(pl.multiple_of(start, FEAT_W), size), :], everyone, ((1,), (1,)))
            e = jnp.exp2(s * LOG2_SCALE - peak)
            at = [slopes[t] + (level + slope_y * (first_line + l).astype(jnp.float32)) for l in range(lines)]
            grad = (e * jnp.concatenate(at, axis=0)).astype(jnp.bfloat16)
            result = dot(grad, everyone, ((1,), (0,)))
            for c in range(tiles):
                place = pl.ds(i * (size * tiles * held) + c * held + t, size, stride=tiles * held)
                out_ref[place, :] = result[:, c * LANES : (c + 1) * LANES]
        return carry

    lax.fori_loop(0, block // size, frame_part, 0)

    mine = term[me_f]
    for d, copy in enumerate(term_copies, 1):
        copy.wait_recv()
        mine += term_in[d]
    query_out_ref[...] = mine
    for copy in sends:
        copy.wait_send()


def on_device(n_track, n_frame, frames, query_frame, query_pixel, cotangent):
    held, pixels, channels = frames.shape
    q = query_frame.shape[0]
    rows = q // n_frame
    block = pixels // n_track
    tiles = channels // LANES
    wide = 4 * LANES
    vmem = pl.BlockSpec(memory_space=pltpu.VMEM)
    dma = pltpu.SemaphoreType.DMA
    frame_grad, query_grad = pl.pallas_call(
        functools.partial(kernel, n_track, n_frame),
        out_shape=(
            jax.ShapeDtypeStruct((block * tiles * held, LANES), jnp.float32),
            jax.ShapeDtypeStruct((rows, channels), jnp.float32),
        ),
        in_specs=[pl.BlockSpec(memory_space=pl.ANY), vmem, vmem, vmem],
        out_specs=(vmem, vmem),
        scratch_shapes=[
            pltpu.VMEM((held, pixels, channels), jnp.bfloat16),
            pltpu.VMEM((held, pixels // wide, q, wide), jnp.float32),
            pltpu.VMEM((n_frame, rows, channels), jnp.bfloat16),
            pltpu.VMEM((n_frame, rows, channels), jnp.bfloat16),
            pltpu.VMEM((n_track, n_frame, rows, channels), jnp.bfloat16),
            pltpu.VMEM((n_track, 4 * held, q), jnp.float32),
            pltpu.VMEM((n_frame, rows, channels), jnp.float32),
            pltpu.VMEM((n_frame, rows, channels), jnp.float32),
            dma((held, 4)),
            dma((n_frame,)),
            dma((n_frame,)),
            dma((n_frame,)),
            dma((n_frame,)),
            dma((n_track,)),
            dma((n_track,)),
            dma((n_track,)),
            dma((n_track,)),
            dma((n_frame,)),
            dma((n_frame,)),
        ],
        compiler_params=pltpu.CompilerParams(
            collective_id=0, has_side_effects=True, vmem_limit_bytes=40 * 2**20
        ),
        name="matching_grad",
    )(frames, query_frame.reshape(1, q), query_pixel.reshape(1, q), cotangent)
    frame_grad = frame_grad.reshape(block, tiles, held, LANES).transpose(0, 2, 1, 3)
    return (frame_grad.reshape(block, held, channels), query_grad)


def solution(mesh):
    return jax.shard_map(
        functools.partial(on_device, mesh.shape["track"], mesh.shape["frame"]),
        mesh=mesh,
        in_specs=(
            P(("groups", "frame"), None, None),
            P(("groups", "track")),
            P(("groups", "track")),
            P(None, ("groups", "frame"), "track"),
        ),
        out_specs=(P("track", ("groups", "frame"), None), P(("groups", "track", "frame"), None)),
        check_vma=False,
    )
```

```python
import functools
import math

import jax
import jax.numpy as jnp
from jax import lax
from jax.experimental import pallas as pl
from jax.experimental.pallas import tpu as pltpu
from jax.sharding import PartitionSpec as P

C = 256
FEAT_H = 64
FEAT_W = 64
LANES = 128
MESH = pl.DeviceIdType.MESH
SCORE_SCALE = C ** (-0.5)
LOG2_SCALE = SCORE_SCALE * math.log2(math.e)
STEP_X = 2.0 / (FEAT_W - 1)
STEP_Y = 2.0 / (FEAT_H - 1)


def dot(a, b, dims):
    return lax.dot_general(a, b, (dims, ((), ())), preferred_element_type=jnp.float32)


def kernel(
    n_track,
    n_frame,
    frames_hbm,
    query_frame_hbm,
    query_pixel_hbm,
    cot_hbm,
    out_hbm,
    query_out_ref,
    fr,
    out_ref,
    out_sem,
    query_frame_ref,
    query_pixel_ref,
    cot_ref,
    small_sem,
    scores,
    picked,
    picked_in,
    feats,
    stats,
    term,
    term_in,
    load_sem,
    pick_send,
    pick_recv,
    ring_send,
    ring_recv,
    feat_send,
    feat_recv,
    stat_send,
    stat_recv,
    term_send,
    term_recv,
):
    held, pixels, channels = fr.shape
    q = cot_ref.shape[2]
    rows = q // n_frame
    block = pixels // n_track
    me_t = lax.axis_index("track")
    me_f = lax.axis_index("frame")

    def peers(name, me, n):
        return [(d, {name: lax.rem(me + d, n)}) for d in range(1, n)]

    track_peers = peers("track", me_t, n_track)
    frame_peers = peers("frame", me_f, n_frame)

    barrier = pltpu.get_barrier_semaphore()
    for _, device in track_peers + frame_peers:
        pl.semaphore_signal(barrier, inc=1, device_id=device, device_id_type=MESH)

    small = [
        pltpu.make_async_copy(src, dst, small_sem.at[i])
        for i, (src, dst) in enumerate(
            [(query_frame_hbm, query_frame_ref), (query_pixel_hbm, query_pixel_ref), (cot_hbm, cot_ref)]
        )
    ]
    for load in small:
        load.start()
    parts = load_sem.shape[1]
    piece = pixels // parts
    loads = []
    for t in range(held):
        for i in range(parts):
            where = pl.ds(i * piece, piece)
            load = pltpu.make_async_copy(frames_hbm.at[t, where], fr.at[t, where], load_sem.at[t, i])
            load.start()
            loads.append((t, i, load))

    eye = lax.broadcasted_iota(jnp.int32, (q, q), 0) == lax.broadcasted_iota(jnp.int32, (q, q), 1)

    def to_column(row):
        return jnp.sum(jnp.where(eye, row, jnp.zeros_like(row)), axis=1, keepdims=True)

    def to_row(column):
        return jnp.sum(jnp.where(eye, column, jnp.zeros_like(column)), axis=0, keepdims=True)

    for load in small:
        load.wait()
    index = (query_frame_ref[...] - me_f * held) * pixels + query_pixel_ref[...]
    index = to_column(index.astype(jnp.float32)).astype(jnp.int32)
    lane = lax.broadcasted_iota(jnp.int32, (q, piece), 1)
    total = jnp.zeros((q, channels), jnp.float32)
    for t, i, load in loads:
        load.wait()
        hot = jnp.where(lane == index - (t * pixels + i * piece), 1.0, 0.0).astype(jnp.bfloat16)
        total += dot(hot, fr[t, i * piece : (i + 1) * piece, :], ((1,), (0,)))
    picked[...] = total.astype(jnp.bfloat16).reshape(n_frame, rows, channels)

    pl.semaphore_wait(barrier, n_track + n_frame - 2)

    copies = []
    for d, device in frame_peers:
        copies.append(
            pltpu.make_async_remote_copy(
                src_ref=picked.at[lax.rem(me_f + d, n_frame)],
                dst_ref=picked_in.at[d],
                send_sem=pick_send.at[d],
                recv_sem=pick_recv.at[d],
                device_id=device,
                device_id_type=MESH,
            )
        )
        copies[-1].start()
    mine = picked[me_f].astype(jnp.float32)
    for d, copy in enumerate(copies, 1):
        copy.wait_recv()
        mine += picked_in[d].astype(jnp.float32)
    feats[me_t, me_f] = mine.astype(jnp.bfloat16)
    sends = copies
    copies = []
    for d, device in frame_peers:
        copies.append(
            pltpu.make_async_remote_copy(
                src_ref=feats.at[me_t, me_f],
                dst_ref=feats.at[me_t, me_f],
                send_sem=ring_send.at[d],
                recv_sem=ring_recv.at[d],
                device_id=device,
                device_id_type=MESH,
            )
        )
        copies[-1].start()
    for copy in copies:
        copy.wait_recv()
    sends += copies
    feat_copies = []
    for d, device in track_peers:
        feat_copies.append(
            pltpu.make_async_remote_copy(
                src_ref=feats.at[me_t],
                dst_ref=feats.at[me_t],
                send_sem=feat_send.at[d],
                recv_sem=feat_recv.at[d],
                device_id=device,
                device_id_type=MESH,
            )
        )
        feat_copies[-1].start()
    sends += feat_copies

    own = feats[me_t].reshape(q, channels)
    wide = scores.shape[3]
    cols = wide // LANES
    chunks = pixels // wide
    lane = lax.broadcasted_iota(jnp.int32, (q, LANES), 1)
    lane_x = (lane % FEAT_W).astype(jnp.float32)
    lane_y = (lane // FEAT_W).astype(jnp.float32)
    row_step = LANES // FEAT_W

    def split(x):
        return [x[:, c * LANES : (c + 1) * LANES] for c in range(cols)]

    def chunk_of(t, i):
        return fr[t, pl.ds(pl.multiple_of(i * wide, wide), wide), :]

    peaks = []
    for t in range(held):

        def score(i, peak):
            s = dot(own, chunk_of(t, i), ((1,), (1,)))
            scores[t, i] = s
            return functools.reduce(jnp.maximum, split(s), peak)

        peak = lax.fori_loop(0, chunks, score, jnp.full((q, LANES), -jnp.inf, jnp.float32), unroll=True)
        peaks.append(jnp.max(peak, axis=1, keepdims=True) * LOG2_SCALE)

    columns = []
    for t in range(held):

        def expo(i, carry):
            zero, first = carry
            e = jnp.exp2(scores[t, i] * LOG2_SCALE - peaks[t])
            scores[t, i] = e
            e = split(e)
            tail = e[-1]
            moment = tail
            for part in e[-2:0:-1]:
                tail = tail + part
                moment = moment + tail
            tail = tail + e[0]
            return zero + tail, first + (moment + tail * (i * cols).astype(jnp.float32))

        empty = jnp.zeros((q, LANES), jnp.float32)
        zero, first = lax.fori_loop(0, chunks, expo, (empty, empty), unroll=4)
        mass = jnp.sum(zero, axis=1, keepdims=True)
        mean_x = jnp.sum(zero * lane_x, axis=1, keepdims=True) / mass
        mean_y = jnp.sum(zero * lane_y + first * row_step, axis=1, keepdims=True) / mass
        grad_x = to_column(cot_ref[0, t : t + 1, :])
        grad_y = to_column(cot_ref[1, t : t + 1, :])
        scale = SCORE_SCALE / mass
        slope_x = grad_x * STEP_X * scale
        slope_y = grad_y * STEP_Y * scale
        columns.append((slope_x, slope_y, -(slope_x * mean_x + slope_y * mean_y)))

    for t in range(held):
        for i, column in enumerate((peaks[t],) + columns[t]):
            stats[me_t, 4 * t + i : 4 * t + i + 1, :] = to_row(column)
    stat_copies = []
    for d, device in track_peers:
        stat_copies.append(
            pltpu.make_async_remote_copy(
                src_ref=stats.at[me_t],
                dst_ref=stats.at[me_t],
                send_sem=stat_send.at[d],
                recv_sem=stat_recv.at[d],
                device_id=device,
                device_id_type=MESH,
            )
        )
        stat_copies[-1].start()
    sends += stat_copies

    total = jnp.zeros((q, channels), jnp.float32)
    for t in range(held):
        slope_x, slope_y, level = columns[t]
        base = level + slope_x * lane_x + slope_y * lane_y
        step = slope_y * row_step

        def query_part(i, total):
            at = [base + step * (i * cols + c).astype(jnp.float32) for c in range(cols)]
            grad = (scores[t, i] * jnp.concatenate(at, axis=1)).astype(jnp.bfloat16)
            return total + dot(grad, chunk_of(t, i), ((1,), (0,)))

        total = lax.fori_loop(0, chunks, query_part, total, unroll=True)
    term[...] = total.reshape(n_frame, rows, channels)
    term_copies = []
    for d, device in frame_peers:
        term_copies.append(
            pltpu.make_async_remote_copy(
                src_ref=term.at[lax.rem(me_f + d, n_frame)],
                dst_ref=term_in.at[d],
                send_sem=term_send.at[d],
                recv_sem=term_recv.at[d],
                device_id=device,
                device_id_type=MESH,
            )
        )
        term_copies[-1].start()
    sends += term_copies

    for copy in feat_copies + stat_copies:
        copy.wait_recv()
    tracks = n_track * q
    everyone = feats[...].reshape(tracks, channels)
    levels = jnp.concatenate([stats[k] for k in range(n_track)], axis=1)
    size = block // out_sem.shape[0]
    lines = size // FEAT_W
    tiles = channels // LANES
    column_x = lax.broadcasted_iota(jnp.int32, (FEAT_W, 1), 0).astype(jnp.float32)
    slopes = [levels[4 * t + 1 : 4 * t + 2] * column_x for t in range(held)]

    def store(i):
        where = pl.ds(i * (size * tiles * held), size * tiles * held)
        return pltpu.make_async_copy(out_ref.at[where], out_hbm.at[where], out_sem.at[i])

    def frame_part(i, carry):
        start = me_t * block + i * size
        first_line = me_t * (block // FEAT_W) + i * lines
        for t in range(held):
            peak, _, slope_y, level = [levels[4 * t + j : 4 * t + j + 1] for j in range(4)]
            s = dot(fr[t, pl.ds(pl.multiple_of(start, FEAT_W), size), :], everyone, ((1,), (1,)))
            e = jnp.exp2(s * LOG2_SCALE - peak)
            at = [slopes[t] + (level + slope_y * (first_line + l).astype(jnp.float32)) for l in range(lines)]
            grad = (e * jnp.concatenate(at, axis=0)).astype(jnp.bfloat16)
            result = dot(grad, everyone, ((1,), (0,)))
            for c in range(tiles):
                place = pl.ds(i * (size * tiles * held) + c * held + t, size, stride=tiles * held)
                out_ref[place, :] = result[:, c * LANES : (c + 1) * LANES]
        store(i).start()
        return carry

    lax.fori_loop(0, block // size, frame_part, 0, unroll=2)

    mine = term[me_f]
    for d, copy in enumerate(term_copies, 1):
        copy.wait_recv()
        mine += term_in[d]
    query_out_ref[...] = mine
    for i in range(block // size):
        store(i).wait()
    for copy in sends:
        copy.wait_send()


def on_device(n_track, n_frame, frames, query_frame, query_pixel, cotangent):
    held, pixels, channels = frames.shape
    q = query_frame.shape[0]
    rows = q // n_frame
    block = pixels // n_track
    tiles = channels // LANES
    wide = 4 * LANES
    size = max(FEAT_W, min(block, 131072 // (n_track * q) // FEAT_W * FEAT_W))
    vmem = pl.BlockSpec(memory_space=pltpu.VMEM)
    dma = pltpu.SemaphoreType.DMA
    frame_grad, query_grad = pl.pallas_call(
        functools.partial(kernel, n_track, n_frame),
        out_shape=(
            jax.ShapeDtypeStruct((block * tiles * held, LANES), jnp.float32),
            jax.ShapeDtypeStruct((rows, channels), jnp.float32),
        ),
        in_specs=[pl.BlockSpec(memory_space=pltpu.HBM)] * 4,
        out_specs=(pl.BlockSpec(memory_space=pltpu.HBM), vmem),
        scratch_shapes=[
            pltpu.VMEM((held, pixels, channels), jnp.bfloat16),
            pltpu.VMEM((block * tiles * held, LANES), jnp.float32),
            dma((block // size,)),
            pltpu.VMEM((1, q), jnp.int32),
            pltpu.VMEM((1, q), jnp.int32),
            pltpu.VMEM(cotangent.shape, jnp.float32),
            dma((3,)),
            pltpu.VMEM((held, pixels // wide, q, wide), jnp.float32),
            pltpu.VMEM((n_frame, rows, channels), jnp.bfloat16),
            pltpu.VMEM((n_frame, rows, channels), jnp.bfloat16),
            pltpu.VMEM((n_track, n_frame, rows, channels), jnp.bfloat16),
            pltpu.VMEM((n_track, 4 * held, q), jnp.float32),
            pltpu.VMEM((n_frame, rows, channels), jnp.float32),
            pltpu.VMEM((n_frame, rows, channels), jnp.float32),
            dma((held, 4)),
            dma((n_frame,)),
            dma((n_frame,)),
            dma((n_frame,)),
            dma((n_frame,)),
            dma((n_track,)),
            dma((n_track,)),
            dma((n_track,)),
            dma((n_track,)),
            dma((n_frame,)),
            dma((n_frame,)),
        ],
        compiler_params=pltpu.CompilerParams(
            collective_id=0, has_side_effects=True, vmem_limit_bytes=64 * 2**20
        ),
        name="matching_grad",
    )(frames, query_frame.reshape(1, q), query_pixel.reshape(1, q), cotangent)
    frame_grad = frame_grad.reshape(block, tiles, held, LANES).transpose(0, 2, 1, 3)
    return (frame_grad.reshape(block, held, channels), query_grad)


def solution(mesh):
    return jax.shard_map(
        functools.partial(on_device, mesh.shape["track"], mesh.shape["frame"]),
        mesh=mesh,
        in_specs=(
            P(("groups", "frame"), None, None),
            P(("groups", "track")),
            P(("groups", "track")),
            P(None, ("groups", "frame"), "track"),
        ),
        out_specs=(P("track", ("groups", "frame"), None), P(("groups", "track", "frame"), None)),
        check_vma=False,
    )
```

```python
import functools

import jax
import jax.numpy as jnp
from jax import lax
from jax.experimental import pallas as pl
from jax.experimental.pallas import tpu as pltpu
from jax.sharding import PartitionSpec as P

C = 256
FEAT_H = 64
FEAT_W = 64
LANES = 128
MESH = pl.DeviceIdType.MESH
SCORE_SCALE = C ** (-0.5)
STEP_X = 2.0 / (FEAT_W - 1)
STEP_Y = 2.0 / (FEAT_H - 1)


def dot(a, b, dims):
    return lax.dot_general(a, b, (dims, ((), ())), preferred_element_type=jnp.float32)


def kernel(
    n_track,
    n_frame,
    frames_hbm,
    small_ref,
    out_ref,
    query_out_ref,
    fr,
    scores,
    picked,
    picked_in,
    feats,
    stats,
    term,
    term_in,
    load_sem,
    pick_send,
    pick_recv,
    ring_send,
    ring_recv,
    feat_send,
    feat_recv,
    stat_send,
    stat_recv,
    term_send,
    term_recv,
):
    held, pixels, channels = fr.shape
    q = small_ref.shape[1]
    rows = q // n_frame
    block = pixels // n_track
    me_t = lax.axis_index("track")
    me_f = lax.axis_index("frame")

    def peers(name, me, n):
        return [(d, {name: lax.rem(me + d, n)}) for d in range(1, n)]

    track_peers = peers("track", me_t, n_track)
    frame_peers = peers("frame", me_f, n_frame)

    barrier = pltpu.get_barrier_semaphore()
    for _, device in track_peers + frame_peers:
        pl.semaphore_signal(barrier, inc=1, device_id=device, device_id_type=MESH)

    parts = load_sem.shape[1]
    piece = pixels // parts
    loads = []
    for t in range(held):
        for i in range(parts):
            where = pl.ds(i * piece, piece)
            load = pltpu.make_async_copy(frames_hbm.at[t, where], fr.at[t, where], load_sem.at[t, i])
            load.start()
            loads.append((t, i, load))

    eye = lax.broadcasted_iota(jnp.int32, (q, q), 0) == lax.broadcasted_iota(jnp.int32, (q, q), 1)

    def to_column(row):
        return jnp.sum(jnp.where(eye, row, jnp.zeros_like(row)), axis=1, keepdims=True)

    def to_row(column):
        return jnp.sum(jnp.where(eye, column, jnp.zeros_like(column)), axis=0, keepdims=True)

    index = (small_ref[2 * held : 2 * held + 1, :].astype(jnp.int32) - me_f * held) * pixels
    index += small_ref[2 * held + 1 : 2 * held + 2, :].astype(jnp.int32)
    index = to_column(index.astype(jnp.float32)).astype(jnp.int32)
    lane = lax.broadcasted_iota(jnp.int32, (q, piece), 1)
    total = jnp.zeros((q, channels), jnp.float32)
    for t, i, load in loads:
        load.wait()
        hot = jnp.where(lane == index - (t * pixels + i * piece), 1.0, 0.0).astype(jnp.bfloat16)
        total += dot(hot, fr[t, i * piece : (i + 1) * piece, :], ((1,), (0,)))
    picked[...] = total.astype(jnp.bfloat16).reshape(n_frame, rows, channels)

    pl.semaphore_wait(barrier, n_track + n_frame - 2)

    copies = []
    for d, device in frame_peers:
        copies.append(
            pltpu.make_async_remote_copy(
                src_ref=picked.at[lax.rem(me_f + d, n_frame)],
                dst_ref=picked_in.at[d],
                send_sem=pick_send.at[d],
                recv_sem=pick_recv.at[d],
                device_id=device,
                device_id_type=MESH,
            )
        )
        copies[-1].start()
    mine = picked[me_f].astype(jnp.float32)
    for d, copy in enumerate(copies, 1):
        copy.wait_recv()
        mine += picked_in[d].astype(jnp.float32)
    feats[me_t, me_f] = mine.astype(jnp.bfloat16)
    sends = copies
    copies = []
    for d, device in frame_peers:
        copies.append(
            pltpu.make_async_remote_copy(
                src_ref=feats.at[me_t, me_f],
                dst_ref=feats.at[me_t, me_f],
                send_sem=ring_send.at[d],
                recv_sem=ring_recv.at[d],
                device_id=device,
                device_id_type=MESH,
            )
        )
        copies[-1].start()
    for copy in copies:
        copy.wait_recv()
    sends += copies
    feat_copies = []
    for d, device in track_peers:
        feat_copies.append(
            pltpu.make_async_remote_copy(
                src_ref=feats.at[me_t],
                dst_ref=feats.at[me_t],
                send_sem=feat_send.at[d],
                recv_sem=feat_recv.at[d],
                device_id=device,
                device_id_type=MESH,
            )
        )
        feat_copies[-1].start()
    sends += feat_copies

    own = feats[me_t].reshape(q, channels)
    wide = scores.shape[3]
    cols = wide // LANES
    chunks = pixels // wide
    lane = lax.broadcasted_iota(jnp.int32, (q, LANES), 1)
    lane_x = (lane % FEAT_W).astype(jnp.float32)
    lane_y = (lane // FEAT_W).astype(jnp.float32)
    row_step = LANES // FEAT_W

    def split(x):
        return [x[:, c * LANES : (c + 1) * LANES] for c in range(cols)]

    def chunk_of(t, i):
        return fr[t, pl.ds(pl.multiple_of(i * wide, wide), wide), :]

    def scores_step(t, i, peak):
        s = dot(own, chunk_of(t, i), ((1,), (1,)))
        scores[t, i] = s
        return functools.reduce(jnp.maximum, split(s), peak)

    def expo_step(t, i, carry):
        zero, first = carry
        e = jnp.exp(scores[t, i] * SCORE_SCALE - peaks[t])
        scores[t, i] = e
        e = split(e)
        tail = e[-1]
        moment = tail
        for part in e[-2:0:-1]:
            tail = tail + part
            moment = moment + tail
        tail = tail + e[0]
        return zero + tail, first + (moment + tail * float(i * cols))

    def query_step(t, i, total):
        slope_x, slope_y, level = columns[t]
        base = level + slope_x * lane_x + slope_y * lane_y
        at = [base + slope_y * float((i * cols + c) * row_step) for c in range(cols)]
        grad = (scores[t, i] * jnp.concatenate(at, axis=1)).astype(jnp.bfloat16)
        return total + dot(grad, chunk_of(t, i), ((1,), (0,)))

    def softmax_terms(t, zero, first):
        mass = jnp.sum(zero, axis=1, keepdims=True)
        mean_x = jnp.sum(zero * lane_x, axis=1, keepdims=True) / mass
        mean_y = jnp.sum(zero * lane_y + first * row_step, axis=1, keepdims=True) / mass
        grad_x = to_column(small_ref[t : t + 1, :])
        grad_y = to_column(small_ref[held + t : held + t + 1, :])
        scale = SCORE_SCALE / mass
        slope_x = grad_x * STEP_X * scale
        slope_y = grad_y * STEP_Y * scale
        return slope_x, slope_y, -(slope_x * mean_x + slope_y * mean_y)

    peaks, columns, stat_copies = {}, {}, []
    total = jnp.zeros((q, channels), jnp.float32)
    empty = jnp.zeros((q, LANES), jnp.float32)
    for turn in range(held + 2):
        peak = jnp.full((q, LANES), -jnp.inf, jnp.float32)
        sums = (empty, empty)
        for i in range(chunks):
            if turn < held:
                peak = scores_step(turn, i, peak)
            if 0 <= turn - 1 < held:
                sums = expo_step(turn - 1, i, sums)
            if 0 <= turn - 2 < held:
                total = query_step(turn - 2, i, total)
        if turn < held:
            peaks[turn] = jnp.max(peak, axis=1, keepdims=True) * SCORE_SCALE
        if 0 <= turn - 1 < held:
            columns[turn - 1] = softmax_terms(turn - 1, *sums)
        if turn == held:
            for t in range(held):
                for i, column in enumerate((peaks[t],) + columns[t]):
                    stats[me_t, 4 * t + i : 4 * t + i + 1, :] = to_row(column)
            for d, device in track_peers:
                stat_copies.append(
                    pltpu.make_async_remote_copy(
                        src_ref=stats.at[me_t],
                        dst_ref=stats.at[me_t],
                        send_sem=stat_send.at[d],
                        recv_sem=stat_recv.at[d],
                        device_id=device,
                        device_id_type=MESH,
                    )
                )
                stat_copies[-1].start()
    sends += stat_copies

    term[...] = total.reshape(n_frame, rows, channels)
    term_copies = []
    for d, device in frame_peers:
        term_copies.append(
            pltpu.make_async_remote_copy(
                src_ref=term.at[lax.rem(me_f + d, n_frame)],
                dst_ref=term_in.at[d],
                send_sem=term_send.at[d],
                recv_sem=term_recv.at[d],
                device_id=device,
                device_id_type=MESH,
            )
        )
        term_copies[-1].start()
    sends += term_copies

    for copy in feat_copies + stat_copies:
        copy.wait_recv()
    tracks = n_track * q
    everyone = feats[...].reshape(tracks, channels)
    levels = jnp.concatenate([stats[k] for k in range(n_track)], axis=1)
    size = max(FEAT_W, min(block, 131072 // tracks // FEAT_W * FEAT_W))
    lines = size // FEAT_W
    tiles = channels // LANES
    column_x = lax.broadcasted_iota(jnp.int32, (FEAT_W, 1), 0).astype(jnp.float32)
    slopes = [levels[4 * t + 1 : 4 * t + 2] * column_x for t in range(held)]

    def frame_part(i, carry):
        start = me_t * block + i * size
        first_line = me_t * (block // FEAT_W) + i * lines
        for t in range(held):
            peak, _, slope_y, level = [levels[4 * t + j : 4 * t + j + 1] for j in range(4)]
            s = dot(fr[t, pl.ds(pl.multiple_of(start, FEAT_W), size), :], everyone, ((1,), (1,)))
            e = jnp.exp(s * SCORE_SCALE - peak)
            at = [slopes[t] + (level + slope_y * (first_line + l).astype(jnp.float32)) for l in range(lines)]
            grad = (e * jnp.concatenate(at, axis=0)).astype(jnp.bfloat16)
            result = dot(grad, everyone, ((1,), (0,)))
            for c in range(tiles):
                place = pl.ds(i * (size * tiles * held) + c * held + t, size, stride=tiles * held)
                out_ref[place, :] = result[:, c * LANES : (c + 1) * LANES]
        return carry

    lax.fori_loop(0, block // size, frame_part, 0, unroll=True)

    mine = term[me_f]
    for d, copy in enumerate(term_copies, 1):
        copy.wait_recv()
        mine += term_in[d]
    query_out_ref[...] = mine
    for copy in sends:
        copy.wait_send()


def on_device(n_track, n_frame, frames, query_frame, query_pixel, cotangent):
    held, pixels, channels = frames.shape
    q = query_frame.shape[0]
    rows = q // n_frame
    block = pixels // n_track
    tiles = channels // LANES
    wide = 4 * LANES
    line = lax.broadcasted_iota(jnp.int32, (2 * held + 2, q), 0)
    small = jnp.pad(cotangent.reshape(2 * held, q), ((0, 2), (0, 0)))
    small = jnp.where(line == 2 * held, query_frame.astype(jnp.float32), small)
    small = jnp.where(line == 2 * held + 1, query_pixel.astype(jnp.float32), small)
    vmem = pl.BlockSpec(memory_space=pltpu.VMEM)
    dma = pltpu.SemaphoreType.DMA
    frame_grad, query_grad = pl.pallas_call(
        functools.partial(kernel, n_track, n_frame),
        out_shape=(
            jax.ShapeDtypeStruct((block * tiles * held, LANES), jnp.float32),
            jax.ShapeDtypeStruct((rows, channels), jnp.float32),
        ),
        in_specs=[pl.BlockSpec(memory_space=pltpu.HBM), vmem],
        out_specs=(vmem, vmem),
        scratch_shapes=[
            pltpu.VMEM((held, pixels, channels), jnp.bfloat16),
            pltpu.VMEM((held, pixels // wide, q, wide), jnp.float32),
            pltpu.VMEM((n_frame, rows, channels), jnp.bfloat16),
            pltpu.VMEM((n_frame, rows, channels), jnp.bfloat16),
            pltpu.VMEM((n_track, n_frame, rows, channels), jnp.bfloat16),
            pltpu.VMEM((n_track, 4 * held, q), jnp.float32),
            pltpu.VMEM((n_frame, rows, channels), jnp.float32),
            pltpu.VMEM((n_frame, rows, channels), jnp.float32),
            dma((held, 4)),
            dma((n_frame,)),
            dma((n_frame,)),
            dma((n_frame,)),
            dma((n_frame,)),
            dma((n_track,)),
            dma((n_track,)),
            dma((n_track,)),
            dma((n_track,)),
            dma((n_frame,)),
            dma((n_frame,)),
        ],
        compiler_params=pltpu.CompilerParams(
            collective_id=0, has_side_effects=True, vmem_limit_bytes=60 * 2**20
        ),
        name="matching_grad",
    )(frames, small)
    frame_grad = frame_grad.reshape(block, tiles, held, LANES).transpose(0, 2, 1, 3)
    return (frame_grad.reshape(block, held, channels), query_grad)


def solution(mesh):
    return jax.shard_map(
        functools.partial(on_device, mesh.shape["track"], mesh.shape["frame"]),
        mesh=mesh,
        in_specs=(
            P(("groups", "frame"), None, None),
            P(("groups", "track")),
            P(("groups", "track")),
            P(None, ("groups", "frame"), "track"),
        ),
        out_specs=(P("track", ("groups", "frame"), None), P(("groups", "track", "frame"), None)),
        check_vma=False,
    )
```

```python
import functools

import jax
import jax.numpy as jnp
from jax import lax
from jax.experimental import pallas as pl
from jax.experimental.pallas import tpu as pltpu
from jax.sharding import PartitionSpec as P

C = 256
FEAT_H = 64
FEAT_W = 64
LANES = 128
MESH = pl.DeviceIdType.MESH
SCORE_SCALE = C ** (-0.5)
STEP_X = 2.0 / (FEAT_W - 1)
STEP_Y = 2.0 / (FEAT_H - 1)


def dot(a, b, dims):
    return lax.dot_general(a, b, (dims, ((), ())), preferred_element_type=jnp.float32)


def kernel(
    n_track,
    n_frame,
    frames_hbm,
    index_ref,
    cot_ref,
    out_ref,
    query_out_ref,
    fr,
    scores,
    picked,
    picked_in,
    feats,
    stats,
    term,
    term_in,
    load_sem,
    pick_send,
    pick_recv,
    ring_send,
    ring_recv,
    feat_send,
    feat_recv,
    stat_send,
    stat_recv,
    term_send,
    term_recv,
):
    held, pixels, channels = fr.shape
    q = index_ref.shape[1]
    rows = q // n_frame
    block = pixels // n_track
    me_t = lax.axis_index("track")
    me_f = lax.axis_index("frame")

    def peers(name, me, n):
        return [(d, {name: lax.rem(me + d, n)}) for d in range(1, n)]

    track_peers = peers("track", me_t, n_track)
    frame_peers = peers("frame", me_f, n_frame)

    barrier = pltpu.get_barrier_semaphore()
    for _, device in track_peers + frame_peers:
        pl.semaphore_signal(barrier, inc=1, device_id=device, device_id_type=MESH)

    parts = load_sem.shape[1]
    piece = pixels // parts
    loads = []
    for t in range(held):
        for i in range(parts):
            where = pl.ds(i * piece, piece)
            load = pltpu.make_async_copy(frames_hbm.at[t, where], fr.at[t, where], load_sem.at[t, i])
            load.start()
            loads.append((t, i, load))

    eye = lax.broadcasted_iota(jnp.int32, (q, q), 0) == lax.broadcasted_iota(jnp.int32, (q, q), 1)

    def to_column(row):
        return jnp.sum(jnp.where(eye, row, jnp.zeros_like(row)), axis=1, keepdims=True)

    def to_row(column):
        return jnp.sum(jnp.where(eye, column, jnp.zeros_like(column)), axis=0, keepdims=True)

    index = to_column(index_ref[...]).astype(jnp.int32) - me_f * (held * pixels)
    lane = lax.broadcasted_iota(jnp.int32, (q, piece), 1)
    total = jnp.zeros((q, channels), jnp.float32)
    for t, i, load in loads:
        load.wait()
        hot = jnp.where(lane == index - (t * pixels + i * piece), 1.0, 0.0).astype(jnp.bfloat16)
        total += dot(hot, fr[t, i * piece : (i + 1) * piece, :], ((1,), (0,)))
    picked[...] = total.astype(jnp.bfloat16).reshape(n_frame, rows, channels)

    pl.semaphore_wait(barrier, n_track + n_frame - 2)

    copies = []
    for d, device in frame_peers:
        copies.append(
            pltpu.make_async_remote_copy(
                src_ref=picked.at[lax.rem(me_f + d, n_frame)],
                dst_ref=picked_in.at[d],
                send_sem=pick_send.at[d],
                recv_sem=pick_recv.at[d],
                device_id=device,
                device_id_type=MESH,
            )
        )
        copies[-1].start()
    mine = picked[me_f].astype(jnp.float32)
    for d, copy in enumerate(copies, 1):
        copy.wait_recv()
        mine += picked_in[d].astype(jnp.float32)
    feats[me_t, me_f] = mine.astype(jnp.bfloat16)
    sends = copies
    copies = []
    for d, device in frame_peers:
        copies.append(
            pltpu.make_async_remote_copy(
                src_ref=feats.at[me_t, me_f],
                dst_ref=feats.at[me_t, me_f],
                send_sem=ring_send.at[d],
                recv_sem=ring_recv.at[d],
                device_id=device,
                device_id_type=MESH,
            )
        )
        copies[-1].start()
    for copy in copies:
        copy.wait_recv()
    sends += copies
    feat_copies = []
    for d, device in track_peers:
        feat_copies.append(
            pltpu.make_async_remote_copy(
                src_ref=feats.at[me_t],
                dst_ref=feats.at[me_t],
                send_sem=feat_send.at[d],
                recv_sem=feat_recv.at[d],
                device_id=device,
                device_id_type=MESH,
            )
        )
        feat_copies[-1].start()
    sends += feat_copies

    own = feats[me_t].reshape(q, channels) * jnp.bfloat16(SCORE_SCALE)
    wide = scores.shape[3]
    cols = wide // LANES
    chunks = pixels // wide
    lane = lax.broadcasted_iota(jnp.int32, (q, LANES), 1)
    lane_x = (lane % FEAT_W).astype(jnp.float32)
    lane_y = (lane // FEAT_W).astype(jnp.float32)
    row_step = LANES // FEAT_W

    def split(x):
        return [x[:, c * LANES : (c + 1) * LANES] for c in range(cols)]

    def chunk_of(t, i):
        return fr[t, pl.ds(pl.multiple_of(i * wide, wide), wide), :]

    def scores_step(t, i, peak):
        s = dot(own, chunk_of(t, i), ((1,), (1,)))
        scores[t, i] = s
        return functools.reduce(jnp.maximum, split(s), peak)

    def expo_step(t, i, carry):
        zero, first = carry
        e = [jnp.exp(part - wide_peaks[t]) for part in split(scores[t, i])]
        scores[t, i] = jnp.concatenate(e, axis=1)
        tail = e[-1]
        moment = tail
        for part in e[-2:0:-1]:
            tail = tail + part
            moment = moment + tail
        tail = tail + e[0]
        return zero + tail, first + (moment + tail * float(i * cols))

    def query_step(t, i, total):
        base, step = lines_of[t]
        grad = [
            (part * (base + step * float(i * cols + c))).astype(jnp.bfloat16)
            for c, part in enumerate(split(scores[t, i]))
        ]
        return total + dot(jnp.concatenate(grad, axis=1), chunk_of(t, i), ((1,), (0,)))

    def softmax_terms(t, zero, first):
        mass = jnp.sum(zero, axis=1, keepdims=True)
        mean_x = jnp.sum(zero * lane_x, axis=1, keepdims=True) / mass
        mean_y = jnp.sum(zero * lane_y + first * row_step, axis=1, keepdims=True) / mass
        grad_x = to_column(cot_ref[0, t : t + 1, :])
        grad_y = to_column(cot_ref[1, t : t + 1, :])
        scale = SCORE_SCALE / mass
        slope_x = grad_x * STEP_X * scale
        slope_y = grad_y * STEP_Y * scale
        return slope_x, slope_y, -(slope_x * mean_x + slope_y * mean_y)

    peaks, wide_peaks, columns, lines_of, stat_copies = {}, {}, {}, {}, []
    total = jnp.zeros((q, channels), jnp.float32)
    empty = jnp.zeros((q, LANES), jnp.float32)
    for turn in range(held + 2):
        peak = jnp.full((q, LANES), -jnp.inf, jnp.float32)
        sums = (empty, empty)
        for i in range(chunks):
            if turn < held:
                peak = scores_step(turn, i, peak)
            if 0 <= turn - 1 < held:
                sums = expo_step(turn - 1, i, sums)
            if 0 <= turn - 2 < held:
                total = query_step(turn - 2, i, total)
        if turn < held:
            peaks[turn] = jnp.max(peak, axis=1, keepdims=True)
            wide_peaks[turn] = jnp.broadcast_to(peaks[turn], (q, LANES))
        if 0 <= turn - 1 < held:
            slope_x, slope_y, level = columns[turn - 1] = softmax_terms(turn - 1, *sums)
            step = jnp.broadcast_to(slope_y, (q, LANES))
            lines_of[turn - 1] = (level + slope_x * lane_x + step * lane_y, step * row_step)
        if turn == held:
            for t in range(held):
                for i, column in enumerate((peaks[t],) + columns[t]):
                    stats[me_t, 4 * t + i : 4 * t + i + 1, :] = to_row(column)
            for d, device in track_peers:
                stat_copies.append(
                    pltpu.make_async_remote_copy(
                        src_ref=stats.at[me_t],
                        dst_ref=stats.at[me_t],
                        send_sem=stat_send.at[d],
                        recv_sem=stat_recv.at[d],
                        device_id=device,
                        device_id_type=MESH,
                    )
                )
                stat_copies[-1].start()
    sends += stat_copies

    term[...] = total.reshape(n_frame, rows, channels)
    term_copies = []
    for d, device in frame_peers:
        term_copies.append(
            pltpu.make_async_remote_copy(
                src_ref=term.at[lax.rem(me_f + d, n_frame)],
                dst_ref=term_in.at[d],
                send_sem=term_send.at[d],
                recv_sem=term_recv.at[d],
                device_id=device,
                device_id_type=MESH,
            )
        )
        term_copies[-1].start()
    sends += term_copies

    for copy in feat_copies + stat_copies:
        copy.wait_recv()
    tracks = n_track * q
    everyone = feats[...].reshape(tracks, channels)
    scaled = everyone * jnp.bfloat16(SCORE_SCALE)
    levels = jnp.concatenate([stats[k] for k in range(n_track)], axis=1)
    size = max(FEAT_W, min(block, 131072 // tracks // FEAT_W * FEAT_W))
    lines = size // FEAT_W
    tiles = channels // LANES
    column_x = lax.broadcasted_iota(jnp.int32, (FEAT_W, 1), 0).astype(jnp.float32)
    slopes = [levels[4 * t + 1 : 4 * t + 2] * column_x for t in range(held)]

    def frame_part(i, carry):
        start = me_t * block + i * size
        first_line = me_t * (block // FEAT_W) + i * lines
        for t in range(held):
            peak, _, slope_y, level = [levels[4 * t + j : 4 * t + j + 1] for j in range(4)]
            s = dot(fr[t, pl.ds(pl.multiple_of(start, FEAT_W), size), :], scaled, ((1,), (1,)))
            e = jnp.exp(s - peak)
            at = [slopes[t] + (level + slope_y * (first_line + l).astype(jnp.float32)) for l in range(lines)]
            grad = (e * jnp.concatenate(at, axis=0)).astype(jnp.bfloat16)
            result = dot(grad, everyone, ((1,), (0,)))
            for c in range(tiles):
                place = pl.ds(i * (size * tiles * held) + c * held + t, size, stride=tiles * held)
                out_ref[place, :] = result[:, c * LANES : (c + 1) * LANES]
        return carry

    lax.fori_loop(0, block // size, frame_part, 0, unroll=True)

    mine = term[me_f]
    for d, copy in enumerate(term_copies, 1):
        copy.wait_recv()
        mine += term_in[d]
    query_out_ref[...] = mine
    for copy in sends:
        copy.wait_send()


def on_device(n_track, n_frame, frames, query_frame, query_pixel, cotangent):
    held, pixels, channels = frames.shape
    q = query_frame.shape[0]
    rows = q // n_frame
    block = pixels // n_track
    tiles = channels // LANES
    wide = 4 * LANES
    index = (query_frame * pixels + query_pixel).astype(jnp.float32).reshape(1, q)
    vmem = pl.BlockSpec(memory_space=pltpu.VMEM)
    dma = pltpu.SemaphoreType.DMA
    frame_grad, query_grad = pl.pallas_call(
        functools.partial(kernel, n_track, n_frame),
        out_shape=(
            jax.ShapeDtypeStruct((block * tiles * held, LANES), jnp.float32),
            jax.ShapeDtypeStruct((rows, channels), jnp.float32),
        ),
        in_specs=[pl.BlockSpec(memory_space=pltpu.HBM), vmem, vmem],
        out_specs=(vmem, vmem),
        scratch_shapes=[
            pltpu.VMEM((held, pixels, channels), jnp.bfloat16),
            pltpu.VMEM((held, pixels // wide, q, wide), jnp.float32),
            pltpu.VMEM((n_frame, rows, channels), jnp.bfloat16),
            pltpu.VMEM((n_frame, rows, channels), jnp.bfloat16),
            pltpu.VMEM((n_track, n_frame, rows, channels), jnp.bfloat16),
            pltpu.VMEM((n_track, 4 * held, q), jnp.float32),
            pltpu.VMEM((n_frame, rows, channels), jnp.float32),
            pltpu.VMEM((n_frame, rows, channels), jnp.float32),
            dma((held, 4)),
            dma((n_frame,)),
            dma((n_frame,)),
            dma((n_frame,)),
            dma((n_frame,)),
            dma((n_track,)),
            dma((n_track,)),
            dma((n_track,)),
            dma((n_track,)),
            dma((n_frame,)),
            dma((n_frame,)),
        ],
        compiler_params=pltpu.CompilerParams(
            collective_id=0, has_side_effects=True, vmem_limit_bytes=56 * 2**20
        ),
        name="matching_grad",
    )(frames, index, cotangent)
    frame_grad = frame_grad.reshape(block, tiles, held, LANES).transpose(0, 2, 1, 3)
    return (frame_grad.reshape(block, held, channels), query_grad)


def solution(mesh):
    return jax.shard_map(
        functools.partial(on_device, mesh.shape["track"], mesh.shape["frame"]),
        mesh=mesh,
        in_specs=(
            P(("groups", "frame"), None, None),
            P(("groups", "track")),
            P(("groups", "track")),
            P(None, ("groups", "frame"), "track"),
        ),
        out_specs=(P("track", ("groups", "frame"), None), P(("groups", "track", "frame"), None)),
        check_vma=False,
    )
```

```python
import functools

import jax
import jax.numpy as jnp
from jax import lax
from jax.experimental import pallas as pl
from jax.experimental.pallas import tpu as pltpu
from jax.sharding import PartitionSpec as P

C = 256
FEAT_H = 64
FEAT_W = 64
LANES = 128
MESH = pl.DeviceIdType.MESH
SCORE_SCALE = C ** (-0.5)
STEP_X = 2.0 / (FEAT_W - 1)
STEP_Y = 2.0 / (FEAT_H - 1)


def dot(a, b, dims):
    return lax.dot_general(a, b, (dims, ((), ())), preferred_element_type=jnp.float32)


def kernel(
    n_track,
    n_frame,
    frames_hbm,
    index_ref,
    cot_ref,
    out_ref,
    query_out_ref,
    fr,
    scores,
    picked,
    picked_in,
    feats,
    stats,
    term,
    term_in,
    load_sem,
    pick_send,
    pick_recv,
    ring_send,
    ring_recv,
    feat_send,
    feat_recv,
    stat_send,
    stat_recv,
    term_send,
    term_recv,
):
    held, pixels, channels = fr.shape
    q = index_ref.shape[1]
    rows = q // n_frame
    block = pixels // n_track
    me_t = lax.axis_index("track")
    me_f = lax.axis_index("frame")

    def peers(name, me, n):
        return [(d, {name: lax.rem(me + d, n)}) for d in range(1, n)]

    track_peers = peers("track", me_t, n_track)
    frame_peers = peers("frame", me_f, n_frame)

    barrier = pltpu.get_barrier_semaphore()
    for _, device in track_peers + frame_peers:
        pl.semaphore_signal(barrier, inc=1, device_id=device, device_id_type=MESH)

    parts = load_sem.shape[1]
    piece = pixels // parts
    loads = []
    for t in range(held):
        for i in range(parts):
            where = pl.ds(i * piece, piece)
            load = pltpu.make_async_copy(frames_hbm.at[t, where], fr.at[t, where], load_sem.at[t, i])
            load.start()
            loads.append((t, i, load))

    eye = lax.broadcasted_iota(jnp.int32, (q, q), 0) == lax.broadcasted_iota(jnp.int32, (q, q), 1)

    def to_column(row):
        return jnp.sum(jnp.where(eye, row, jnp.zeros_like(row)), axis=1, keepdims=True)

    def to_row(column):
        return jnp.sum(jnp.where(eye, column, jnp.zeros_like(column)), axis=0, keepdims=True)

    index = to_column(index_ref[...]).astype(jnp.int32) - me_f * (held * pixels)
    lane = lax.broadcasted_iota(jnp.int32, (q, piece), 1)
    total = jnp.zeros((q, channels), jnp.float32)
    for t, i, load in loads:
        load.wait()
        hot = jnp.where(lane == index - (t * pixels + i * piece), 1.0, 0.0).astype(jnp.bfloat16)
        total += dot(hot, fr[t, i * piece : (i + 1) * piece, :], ((1,), (0,)))
    picked[...] = total.astype(jnp.bfloat16).reshape(n_frame, rows, channels)

    pl.semaphore_wait(barrier, n_track + n_frame - 2)

    copies = []
    for d, device in frame_peers:
        copies.append(
            pltpu.make_async_remote_copy(
                src_ref=picked.at[lax.rem(me_f + d, n_frame)],
                dst_ref=picked_in.at[d],
                send_sem=pick_send.at[d],
                recv_sem=pick_recv.at[d],
                device_id=device,
                device_id_type=MESH,
            )
        )
        copies[-1].start()
    mine = picked[me_f].astype(jnp.float32)
    for d, copy in enumerate(copies, 1):
        copy.wait_recv()
        mine += picked_in[d].astype(jnp.float32)
    feats[me_t, me_f] = mine.astype(jnp.bfloat16)
    sends = copies
    copies = []
    for d, device in frame_peers:
        copies.append(
            pltpu.make_async_remote_copy(
                src_ref=feats.at[me_t, me_f],
                dst_ref=feats.at[me_t, me_f],
                send_sem=ring_send.at[d],
                recv_sem=ring_recv.at[d],
                device_id=device,
                device_id_type=MESH,
            )
        )
        copies[-1].start()
    for copy in copies:
        copy.wait_recv()
    sends += copies
    feat_copies = []
    for d, device in track_peers:
        feat_copies.append(
            pltpu.make_async_remote_copy(
                src_ref=feats.at[me_t],
                dst_ref=feats.at[me_t],
                send_sem=feat_send.at[d],
                recv_sem=feat_recv.at[d],
                device_id=device,
                device_id_type=MESH,
            )
        )
        feat_copies[-1].start()
    sends += feat_copies

    own = feats[me_t].reshape(q, channels) * jnp.bfloat16(SCORE_SCALE)
    wide = scores.shape[3]
    cols = wide // LANES
    chunks = pixels // wide
    lane = lax.broadcasted_iota(jnp.int32, (q, LANES), 1)
    lane_x = (lane % FEAT_W).astype(jnp.float32)
    lane_y = (lane // FEAT_W).astype(jnp.float32)
    row_step = LANES // FEAT_W

    def split(x):
        return [x[:, c * LANES : (c + 1) * LANES] for c in range(cols)]

    def chunk_of(t, i):
        return fr[t, pl.ds(pl.multiple_of(i * wide, wide), wide), :]

    def scores_step(t, i, peak):
        s = dot(own, chunk_of(t, i), ((1,), (1,)))
        scores[t, i] = s
        return functools.reduce(jnp.maximum, split(s), peak)

    def expo_step(t, i, carry):
        zero, first = carry
        e = [jnp.exp(part - wide_peaks[t]) for part in split(scores[t, i])]
        scores[t, i] = jnp.concatenate(e, axis=1)
        tail = e[-1]
        moment = tail
        for part in e[-2:0:-1]:
            tail = tail + part
            moment = moment + tail
        tail = tail + e[0]
        return zero + tail, first + (moment + tail * float(i * cols))

    def query_step(t, i, total):
        base, step = lines_of[t]
        grad = [
            (part * (base + step * float(i * cols + c))).astype(jnp.bfloat16)
            for c, part in enumerate(split(scores[t, i]))
        ]
        return total + dot(jnp.concatenate(grad, axis=1), chunk_of(t, i), ((1,), (0,)))

    def softmax_terms(t, zero, first):
        mass = jnp.sum(zero, axis=1, keepdims=True)
        mean_x = jnp.sum(zero * lane_x, axis=1, keepdims=True) / mass
        mean_y = jnp.sum(zero * lane_y + first * row_step, axis=1, keepdims=True) / mass
        grad_x = to_column(cot_ref[0, t : t + 1, :])
        grad_y = to_column(cot_ref[1, t : t + 1, :])
        scale = SCORE_SCALE / mass
        slope_x = grad_x * STEP_X * scale
        slope_y = grad_y * STEP_Y * scale
        return slope_x, slope_y, -(slope_x * mean_x + slope_y * mean_y)

    peaks, wide_peaks, columns, lines_of, stat_copies = {}, {}, {}, {}, []
    total = jnp.zeros((q, channels), jnp.float32)
    empty = jnp.zeros((q, LANES), jnp.float32)
    for turn in range(held + 2):
        peak = jnp.full((q, LANES), -jnp.inf, jnp.float32)
        sums = (empty, empty)
        for i in range(chunks):
            if turn < held:
                peak = scores_step(turn, i, peak)
            if 0 <= turn - 1 < held:
                sums = expo_step(turn - 1, i, sums)
            if 0 <= turn - 2 < held:
                total = query_step(turn - 2, i, total)
        if turn < held:
            peaks[turn] = jnp.max(peak, axis=1, keepdims=True)
            wide_peaks[turn] = jnp.broadcast_to(peaks[turn], (q, LANES))
        if 0 <= turn - 1 < held:
            slope_x, slope_y, level = columns[turn - 1] = softmax_terms(turn - 1, *sums)
            step = jnp.broadcast_to(slope_y, (q, LANES))
            lines_of[turn - 1] = (level + slope_x * lane_x + step * lane_y, step * row_step)
        if turn == held:
            for t in range(held):
                for i, column in enumerate((peaks[t],) + columns[t]):
                    stats[me_t, 4 * t + i : 4 * t + i + 1, :] = to_row(column)
            for d, device in track_peers:
                stat_copies.append(
                    pltpu.make_async_remote_copy(
                        src_ref=stats.at[me_t],
                        dst_ref=stats.at[me_t],
                        send_sem=stat_send.at[d],
                        recv_sem=stat_recv.at[d],
                        device_id=device,
                        device_id_type=MESH,
                    )
                )
                stat_copies[-1].start()
    sends += stat_copies

    term[...] = total.reshape(n_frame, rows, channels)
    term_copies = []
    for d, device in frame_peers:
        term_copies.append(
            pltpu.make_async_remote_copy(
                src_ref=term.at[lax.rem(me_f + d, n_frame)],
                dst_ref=term_in.at[d],
                send_sem=term_send.at[d],
                recv_sem=term_recv.at[d],
                device_id=device,
                device_id_type=MESH,
            )
        )
        term_copies[-1].start()
    sends += term_copies

    for copy in feat_copies + stat_copies:
        copy.wait_recv()
    tracks = n_track * q
    everyone = feats[...].reshape(tracks, channels)
    scaled = everyone * jnp.bfloat16(SCORE_SCALE)
    levels = jnp.concatenate([stats[k] for k in range(n_track)], axis=1)
    size = max(FEAT_W, min(block, 131072 // tracks // FEAT_W * FEAT_W))
    lines = size // FEAT_W
    tiles = channels // LANES
    column_x = lax.broadcasted_iota(jnp.int32, (FEAT_W, 1), 0).astype(jnp.float32)
    slopes = [levels[4 * t + 1 : 4 * t + 2] * column_x for t in range(held)]

    def frame_part(i, carry):
        start = me_t * block + i * size
        first_line = me_t * (block // FEAT_W) + i * lines
        for t in range(held):
            peak, _, slope_y, level = [levels[4 * t + j : 4 * t + j + 1] for j in range(4)]
            s = dot(fr[t, pl.ds(pl.multiple_of(start, FEAT_W), size), :], scaled, ((1,), (1,)))
            e = jnp.exp(s - peak)
            at = [slopes[t] + (level + slope_y * (first_line + l).astype(jnp.float32)) for l in range(lines)]
            grad = (e * jnp.concatenate(at, axis=0)).astype(jnp.bfloat16)
            result = dot(grad, everyone, ((1,), (0,)))
            for c in range(tiles):
                place = pl.ds(i * (size * tiles * held) + c * held + t, size, stride=tiles * held)
                out_ref[place, :] = result[:, c * LANES : (c + 1) * LANES]
        return carry

    lax.fori_loop(0, block // size, frame_part, 0, unroll=True)

    mine = term[me_f]
    for d, copy in enumerate(term_copies, 1):
        copy.wait_recv()
        mine += term_in[d]
    query_out_ref[...] = mine
    for copy in sends:
        copy.wait_send()


def on_device(n_track, n_frame, frames, query_frame, query_pixel, cotangent):
    held, pixels, channels = frames.shape
    q = query_frame.shape[0]
    rows = q // n_frame
    block = pixels // n_track
    tiles = channels // LANES
    wide = 4 * LANES
    index = (query_frame * pixels + query_pixel).astype(jnp.float32).reshape(1, q)
    vmem = pl.BlockSpec(memory_space=pltpu.VMEM)
    dma = pltpu.SemaphoreType.DMA
    frame_grad, query_grad = pl.pallas_call(
        functools.partial(kernel, n_track, n_frame),
        out_shape=(
            jax.ShapeDtypeStruct((block * tiles * held, LANES), jnp.float32),
            jax.ShapeDtypeStruct((rows, channels), jnp.float32),
        ),
        in_specs=[pl.BlockSpec(memory_space=pltpu.HBM), vmem, vmem],
        out_specs=(vmem, vmem),
        scratch_shapes=[
            pltpu.VMEM((held, pixels, channels), jnp.bfloat16),
            pltpu.VMEM((held, pixels // wide, q, wide), jnp.float32),
            pltpu.VMEM((n_frame, rows, channels), jnp.bfloat16),
            pltpu.VMEM((n_frame, rows, channels), jnp.bfloat16),
            pltpu.VMEM((n_track, n_frame, rows, channels), jnp.bfloat16),
            pltpu.VMEM((n_track, 4 * held, q), jnp.float32),
            pltpu.VMEM((n_frame, rows, channels), jnp.float32),
            pltpu.VMEM((n_frame, rows, channels), jnp.float32),
            dma((held, 4)),
            dma((n_frame,)),
            dma((n_frame,)),
            dma((n_frame,)),
            dma((n_frame,)),
            dma((n_track,)),
            dma((n_track,)),
            dma((n_track,)),
            dma((n_track,)),
            dma((n_frame,)),
            dma((n_frame,)),
        ],
        compiler_params=pltpu.CompilerParams(
            collective_id=0, has_side_effects=True, vmem_limit_bytes=48 * 2**20
        ),
        name="matching_grad",
    )(frames, index, cotangent)
    frame_grad = frame_grad.reshape(block, tiles, held, LANES).transpose(0, 2, 1, 3)
    return (frame_grad.reshape(block, held, channels), query_grad)


def solution(mesh):
    return jax.shard_map(
        functools.partial(on_device, mesh.shape["track"], mesh.shape["frame"]),
        mesh=mesh,
        in_specs=(
            P(("groups", "frame"), None, None),
            P(("groups", "track")),
            P(("groups", "track")),
            P(None, ("groups", "frame"), "track"),
        ),
        out_specs=(P("track", ("groups", "frame"), None), P(("groups", "track", "frame"), None)),
        check_vma=False,
    )
```

```python
import functools

import jax
import jax.numpy as jnp
from jax import lax
from jax.experimental import pallas as pl
from jax.experimental.pallas import tpu as pltpu
from jax.sharding import PartitionSpec as P

C = 256
FEAT_H = 64
FEAT_W = 64
LANES = 128
MESH = pl.DeviceIdType.MESH
SCORE_SCALE = C ** (-0.5)
STEP_X = 2.0 / (FEAT_W - 1)
STEP_Y = 2.0 / (FEAT_H - 1)


def dot(a, b, dims):
    return lax.dot_general(a, b, (dims, ((), ())), preferred_element_type=jnp.float32)


def kernel(
    n_track,
    n_frame,
    frames_hbm,
    index_ref,
    cot_ref,
    out_ref,
    query_out_ref,
    fr,
    scores,
    picked,
    picked_in,
    feats,
    stats,
    term,
    term_in,
    load_sem,
    pick_send,
    pick_recv,
    ring_send,
    ring_recv,
    feat_send,
    feat_recv,
    stat_send,
    stat_recv,
    term_send,
    term_recv,
):
    held, pixels, channels = fr.shape
    q = index_ref.shape[1]
    rows = q // n_frame
    block = pixels // n_track
    me_t = lax.axis_index("track")
    me_f = lax.axis_index("frame")

    def peers(name, me, n):
        return [(d, {name: lax.rem(me + d, n)}) for d in range(1, n)]

    track_peers = peers("track", me_t, n_track)
    frame_peers = peers("frame", me_f, n_frame)

    barrier = pltpu.get_barrier_semaphore()
    for _, device in track_peers + frame_peers:
        pl.semaphore_signal(barrier, inc=1, device_id=device, device_id_type=MESH)

    parts = load_sem.shape[1]
    piece = pixels // parts
    loads = []
    for t in range(held):
        for i in range(parts):
            where = pl.ds(i * piece, piece)
            load = pltpu.make_async_copy(frames_hbm.at[t, where], fr.at[t, where], load_sem.at[t, i])
            load.start()
            loads.append((t, i, load))

    eye = lax.broadcasted_iota(jnp.int32, (q, q), 0) == lax.broadcasted_iota(jnp.int32, (q, q), 1)

    def to_column(row):
        return jnp.sum(jnp.where(eye, row, jnp.zeros_like(row)), axis=1, keepdims=True)

    def to_row(column):
        return jnp.sum(jnp.where(eye, column, jnp.zeros_like(column)), axis=0, keepdims=True)

    index = to_column(index_ref[...]).astype(jnp.int32) - me_f * (held * pixels)
    lane = lax.broadcasted_iota(jnp.int32, (q, piece), 1)
    total = jnp.zeros((q, channels), jnp.float32)
    for t, i, load in loads:
        load.wait()
        hot = jnp.where(lane == index - (t * pixels + i * piece), 1.0, 0.0).astype(jnp.bfloat16)
        total += dot(hot, fr[t, i * piece : (i + 1) * piece, :], ((1,), (0,)))
    picked[...] = total.astype(jnp.bfloat16).reshape(n_frame, rows, channels)

    pl.semaphore_wait(barrier, n_track + n_frame - 2)

    copies = []
    for d, device in frame_peers:
        copies.append(
            pltpu.make_async_remote_copy(
                src_ref=picked.at[lax.rem(me_f + d, n_frame)],
                dst_ref=picked_in.at[d],
                send_sem=pick_send.at[d],
                recv_sem=pick_recv.at[d],
                device_id=device,
                device_id_type=MESH,
            )
        )
        copies[-1].start()
    mine = picked[me_f].astype(jnp.float32)
    for d, copy in enumerate(copies, 1):
        copy.wait_recv()
        mine += picked_in[d].astype(jnp.float32)
    feats[me_t, me_f] = mine.astype(jnp.bfloat16)
    sends = copies
    copies = []
    for d, device in frame_peers:
        copies.append(
            pltpu.make_async_remote_copy(
                src_ref=feats.at[me_t, me_f],
                dst_ref=feats.at[me_t, me_f],
                send_sem=ring_send.at[d],
                recv_sem=ring_recv.at[d],
                device_id=device,
                device_id_type=MESH,
            )
        )
        copies[-1].start()
    for copy in copies:
        copy.wait_recv()
    sends += copies
    feat_copies = []
    for d, device in track_peers:
        feat_copies.append(
            pltpu.make_async_remote_copy(
                src_ref=feats.at[me_t],
                dst_ref=feats.at[me_t],
                send_sem=feat_send.at[d],
                recv_sem=feat_recv.at[d],
                device_id=device,
                device_id_type=MESH,
            )
        )
        feat_copies[-1].start()
    sends += feat_copies

    own = feats[me_t].reshape(q, channels) * jnp.bfloat16(SCORE_SCALE)
    wide = scores.shape[3]
    cols = wide // LANES
    chunks = pixels // wide
    lane = lax.broadcasted_iota(jnp.int32, (q, LANES), 1)
    lane_x = (lane % FEAT_W).astype(jnp.float32)
    lane_y = (lane // FEAT_W).astype(jnp.float32)
    row_step = LANES // FEAT_W

    def split(x):
        return [x[:, c * LANES : (c + 1) * LANES] for c in range(cols)]

    def chunk_of(t, i):
        return fr[t, pl.ds(pl.multiple_of(i * wide, wide), wide), :]

    def scores_step(t, i, peak):
        s = dot(own, chunk_of(t, i), ((1,), (1,)))
        scores[t, i] = s
        return functools.reduce(jnp.maximum, split(s), peak)

    def expo_step(t, i, carry):
        zero, first = carry
        e = [jnp.exp(part - wide_peaks[t]) for part in split(scores[t, i])]
        scores[t, i] = jnp.concatenate(e, axis=1)
        tail = e[-1]
        moment = tail
        for part in e[-2:0:-1]:
            tail = tail + part
            moment = moment + tail
        tail = tail + e[0]
        return zero + tail, first + (moment + tail * float(i * cols))

    def query_step(t, i, total):
        base, step = lines_of[t]
        grad = [
            (part * (base + step * float(i * cols + c))).astype(jnp.bfloat16)
            for c, part in enumerate(split(scores[t, i]))
        ]
        return total + dot(jnp.concatenate(grad, axis=1), chunk_of(t, i), ((1,), (0,)))

    def softmax_terms(t, zero, first):
        mass = jnp.sum(zero, axis=1, keepdims=True)
        mean_x = jnp.sum(zero * lane_x, axis=1, keepdims=True) / mass
        mean_y = jnp.sum(zero * lane_y + first * row_step, axis=1, keepdims=True) / mass
        grad_x = to_column(cot_ref[0, t : t + 1, :])
        grad_y = to_column(cot_ref[1, t : t + 1, :])
        scale = SCORE_SCALE / mass
        slope_x = grad_x * STEP_X * scale
        slope_y = grad_y * STEP_Y * scale
        return slope_x, slope_y, -(slope_x * mean_x + slope_y * mean_y)

    peaks, wide_peaks, columns, lines_of, stat_copies = {}, {}, {}, {}, []
    total = jnp.zeros((q, channels), jnp.float32)
    empty = jnp.zeros((q, LANES), jnp.float32)
    for turn in range(held + 2):
        peak = jnp.full((q, LANES), -jnp.inf, jnp.float32)
        sums = (empty, empty)
        for i in range(chunks):
            if turn < held:
                peak = scores_step(turn, i, peak)
            if 0 <= turn - 1 < held:
                sums = expo_step(turn - 1, i, sums)
            if 0 <= turn - 2 < held:
                total = query_step(turn - 2, i, total)
        if turn < held:
            peaks[turn] = jnp.max(peak, axis=1, keepdims=True)
            wide_peaks[turn] = jnp.broadcast_to(peaks[turn], (q, LANES))
        if 0 <= turn - 1 < held:
            slope_x, slope_y, level = columns[turn - 1] = softmax_terms(turn - 1, *sums)
            step = jnp.broadcast_to(slope_y, (q, LANES))
            lines_of[turn - 1] = (level + slope_x * lane_x + step * lane_y, step * row_step)
            rest = [to_row(column) for column in (peaks[turn - 1],) + columns[turn - 1]]
            stats[turn - 1, me_t] = jnp.concatenate(rest + rest, axis=0)
            for d, device in track_peers:
                copy = pltpu.make_async_remote_copy(
                    src_ref=stats.at[turn - 1, me_t],
                    dst_ref=stats.at[turn - 1, me_t],
                    send_sem=stat_send.at[turn - 1, d],
                    recv_sem=stat_recv.at[turn - 1, d],
                    device_id=device,
                    device_id_type=MESH,
                )
                copy.start()
                stat_copies.append(copy)
    sends += stat_copies

    term[...] = total.reshape(n_frame, rows, channels)
    term_copies = []
    for d, device in frame_peers:
        term_copies.append(
            pltpu.make_async_remote_copy(
                src_ref=term.at[lax.rem(me_f + d, n_frame)],
                dst_ref=term_in.at[d],
                send_sem=term_send.at[d],
                recv_sem=term_recv.at[d],
                device_id=device,
                device_id_type=MESH,
            )
        )
        term_copies[-1].start()
    sends += term_copies

    for copy in feat_copies:
        copy.wait_recv()
    tracks = n_track * q
    everyone = feats[...].reshape(tracks, channels)
    scaled = everyone * jnp.bfloat16(SCORE_SCALE)
    size = max(FEAT_W, min(block, 131072 // tracks // FEAT_W * FEAT_W))
    lines = size // FEAT_W
    tiles = channels // LANES
    column_x = lax.broadcasted_iota(jnp.int32, (FEAT_W, 1), 0).astype(jnp.float32)

    for t in range(held):
        for copy in stat_copies[t * (n_track - 1) : (t + 1) * (n_track - 1)]:
            copy.wait_recv()
        levels = jnp.concatenate([stats[t, k] for k in range(n_track)], axis=1)
        peak, slope_x, slope_y, level = [levels[j : j + 1] for j in range(4)]
        slope_x = slope_x * column_x

        def frame_part(i, carry):
            start = me_t * block + i * size
            first_line = me_t * (block // FEAT_W) + i * lines
            s = dot(fr[t, pl.ds(pl.multiple_of(start, FEAT_W), size), :], scaled, ((1,), (1,)))
            e = jnp.exp(s - peak)
            at = [slope_x + (level + slope_y * (first_line + l).astype(jnp.float32)) for l in range(lines)]
            grad = (e * jnp.concatenate(at, axis=0)).astype(jnp.bfloat16)
            result = dot(grad, everyone, ((1,), (0,)))
            for c in range(tiles):
                place = pl.ds(i * (size * tiles * held) + c * held + t, size, stride=tiles * held)
                out_ref[place, :] = result[:, c * LANES : (c + 1) * LANES]
            return carry

        lax.fori_loop(0, block // size, frame_part, 0, unroll=True)

    mine = term[me_f]
    for d, copy in enumerate(term_copies, 1):
        copy.wait_recv()
        mine += term_in[d]
    query_out_ref[...] = mine
    for copy in sends:
        copy.wait_send()


def on_device(n_track, n_frame, frames, query_frame, query_pixel, cotangent):
    held, pixels, channels = frames.shape
    q = query_frame.shape[0]
    rows = q // n_frame
    block = pixels // n_track
    tiles = channels // LANES
    wide = 4 * LANES
    index = (query_frame * pixels + query_pixel).astype(jnp.float32).reshape(1, q)
    vmem = pl.BlockSpec(memory_space=pltpu.VMEM)
    dma = pltpu.SemaphoreType.DMA
    frame_grad, query_grad = pl.pallas_call(
        functools.partial(kernel, n_track, n_frame),
        out_shape=(
            jax.ShapeDtypeStruct((block * tiles * held, LANES), jnp.float32),
            jax.ShapeDtypeStruct((rows, channels), jnp.float32),
        ),
        in_specs=[pl.BlockSpec(memory_space=pltpu.HBM), vmem, vmem],
        out_specs=(vmem, vmem),
        scratch_shapes=[
            pltpu.VMEM((held, pixels, channels), jnp.bfloat16),
            pltpu.VMEM((held, pixels // wide, q, wide), jnp.float32),
            pltpu.VMEM((n_frame, rows, channels), jnp.bfloat16),
            pltpu.VMEM((n_frame, rows, channels), jnp.bfloat16),
            pltpu.VMEM((n_track, n_frame, rows, channels), jnp.bfloat16),
            pltpu.VMEM((held, n_track, 8, q), jnp.float32),
            pltpu.VMEM((n_frame, rows, channels), jnp.float32),
            pltpu.VMEM((n_frame, rows, channels), jnp.float32),
            dma((held, 4)),
            dma((n_frame,)),
            dma((n_frame,)),
            dma((n_frame,)),
            dma((n_frame,)),
            dma((n_track,)),
            dma((n_track,)),
            dma((held, n_track)),
            dma((held, n_track)),
            dma((n_frame,)),
            dma((n_frame,)),
        ],
        compiler_params=pltpu.CompilerParams(
            collective_id=0, has_side_effects=True, vmem_limit_bytes=48 * 2**20
        ),
        name="matching_grad",
    )(frames, index, cotangent)
    frame_grad = frame_grad.reshape(block, tiles, held, LANES).transpose(0, 2, 1, 3)
    return (frame_grad.reshape(block, held, channels), query_grad)


def solution(mesh):
    return jax.shard_map(
        functools.partial(on_device, mesh.shape["track"], mesh.shape["frame"]),
        mesh=mesh,
        in_specs=(
            P(("groups", "frame"), None, None),
            P(("groups", "track")),
            P(("groups", "track")),
            P(None, ("groups", "frame"), "track"),
        ),
        out_specs=(P("track", ("groups", "frame"), None), P(("groups", "track", "frame"), None)),
        check_vma=False,
    )
```

```python
import functools

import jax
import jax.numpy as jnp
from jax import lax
from jax.experimental import pallas as pl
from jax.experimental.pallas import tpu as pltpu
from jax.sharding import PartitionSpec as P

C = 256
FEAT_H = 64
FEAT_W = 64
LANES = 128
MESH = pl.DeviceIdType.MESH
SCORE_SCALE = C ** (-0.5)
STEP_X = 2.0 / (FEAT_W - 1)
STEP_Y = 2.0 / (FEAT_H - 1)


def dot(a, b, dims):
    return lax.dot_general(a, b, (dims, ((), ())), preferred_element_type=jnp.float32)


def kernel(
    n_track,
    n_frame,
    frames_hbm,
    index_ref,
    cot_ref,
    out_ref,
    query_out_ref,
    fr,
    scores,
    picked,
    picked_in,
    feats,
    stats,
    term,
    term_in,
    load_sem,
    pick_send,
    pick_recv,
    feat_send,
    feat_recv,
    stat_send,
    stat_recv,
    term_send,
    term_recv,
):
    held, pixels, channels = fr.shape
    q = index_ref.shape[1]
    rows = q // n_frame
    block = pixels // n_track
    me_t = lax.axis_index("track")
    me_f = lax.axis_index("frame")

    def peers(name, me, n):
        return [(d, {name: lax.rem(me + d, n)}) for d in range(1, n)]

    track_peers = peers("track", me_t, n_track)
    frame_peers = peers("frame", me_f, n_frame)

    barrier = pltpu.get_barrier_semaphore()
    for _, device in track_peers + frame_peers:
        pl.semaphore_signal(barrier, inc=1, device_id=device, device_id_type=MESH)

    parts = load_sem.shape[1]
    piece = pixels // parts
    loads = []
    for t in range(held):
        for i in range(parts):
            where = pl.ds(i * piece, piece)
            load = pltpu.make_async_copy(frames_hbm.at[t, where], fr.at[t, where], load_sem.at[t, i])
            load.start()
            loads.append((t, i, load))

    eye = lax.broadcasted_iota(jnp.int32, (q, q), 0) == lax.broadcasted_iota(jnp.int32, (q, q), 1)

    def to_column(row):
        return jnp.sum(jnp.where(eye, row, jnp.zeros_like(row)), axis=1, keepdims=True)

    def to_row(column):
        return jnp.sum(jnp.where(eye, column, jnp.zeros_like(column)), axis=0, keepdims=True)

    index = to_column(index_ref[...]).astype(jnp.int32) - me_f * (held * pixels)
    lane = lax.broadcasted_iota(jnp.int32, (q, piece), 1)
    total = jnp.zeros((q, channels), jnp.float32)
    for t, i, load in loads:
        load.wait()
        hot = jnp.where(lane == index - (t * pixels + i * piece), 1.0, 0.0).astype(jnp.bfloat16)
        total += dot(hot, fr[t, i * piece : (i + 1) * piece, :], ((1,), (0,)))
    picked[...] = total.astype(jnp.bfloat16).reshape(n_frame, rows, channels)

    pl.semaphore_wait(barrier, n_track + n_frame - 2)

    copies = []
    for d, device in frame_peers:
        copies.append(
            pltpu.make_async_remote_copy(
                src_ref=picked,
                dst_ref=picked_in.at[d],
                send_sem=pick_send.at[d],
                recv_sem=pick_recv.at[d],
                device_id=device,
                device_id_type=MESH,
            )
        )
        copies[-1].start()
    mine = picked[...].astype(jnp.float32)
    for d, copy in enumerate(copies, 1):
        copy.wait_recv()
        mine += picked_in[d].astype(jnp.float32)
    feats[me_t] = mine.astype(jnp.bfloat16)
    sends = copies
    feat_copies = []
    for d, device in track_peers:
        feat_copies.append(
            pltpu.make_async_remote_copy(
                src_ref=feats.at[me_t],
                dst_ref=feats.at[me_t],
                send_sem=feat_send.at[d],
                recv_sem=feat_recv.at[d],
                device_id=device,
                device_id_type=MESH,
            )
        )
        feat_copies[-1].start()
    sends += feat_copies

    own = feats[me_t].reshape(q, channels) * jnp.bfloat16(SCORE_SCALE)
    wide = scores.shape[3]
    cols = wide // LANES
    chunks = pixels // wide
    lane = lax.broadcasted_iota(jnp.int32, (q, LANES), 1)
    lane_x = (lane % FEAT_W).astype(jnp.float32)
    lane_y = (lane // FEAT_W).astype(jnp.float32)
    row_step = LANES // FEAT_W

    def split(x):
        return [x[:, c * LANES : (c + 1) * LANES] for c in range(cols)]

    def chunk_of(t, i):
        return fr[t, pl.ds(pl.multiple_of(i * wide, wide), wide), :]

    def scores_step(t, i, peak):
        s = dot(own, chunk_of(t, i), ((1,), (1,)))
        scores[t, i] = s
        return functools.reduce(jnp.maximum, split(s), peak)

    def expo_step(t, i, carry):
        zero, first = carry
        e = [jnp.exp(part - wide_peaks[t]) for part in split(scores[t, i])]
        scores[t, i] = jnp.concatenate(e, axis=1)
        tail = e[-1]
        moment = tail
        for part in e[-2:0:-1]:
            tail = tail + part
            moment = moment + tail
        tail = tail + e[0]
        return zero + tail, first + (moment + tail * float(i * cols))

    def query_step(t, i, total):
        base, step = lines_of[t]
        grad = [
            (part * (base + step * float(i * cols + c))).astype(jnp.bfloat16)
            for c, part in enumerate(split(scores[t, i]))
        ]
        return total + dot(jnp.concatenate(grad, axis=1), chunk_of(t, i), ((1,), (0,)))

    def softmax_terms(t, zero, first):
        mass = jnp.sum(zero, axis=1, keepdims=True)
        mean_x = jnp.sum(zero * lane_x, axis=1, keepdims=True) / mass
        mean_y = jnp.sum(zero * lane_y + first * row_step, axis=1, keepdims=True) / mass
        grad_x = to_column(cot_ref[0, t : t + 1, :])
        grad_y = to_column(cot_ref[1, t : t + 1, :])
        scale = SCORE_SCALE / mass
        slope_x = grad_x * STEP_X * scale
        slope_y = grad_y * STEP_Y * scale
        return slope_x, slope_y, -(slope_x * mean_x + slope_y * mean_y)

    peaks, wide_peaks, columns, lines_of, stat_copies = {}, {}, {}, {}, []
    total = jnp.zeros((q, channels), jnp.float32)
    empty = jnp.zeros((q, LANES), jnp.float32)
    for turn in range(held + 2):
        peak = jnp.full((q, LANES), -jnp.inf, jnp.float32)
        sums = (empty, empty)
        for i in range(chunks):
            if turn < held:
                peak = scores_step(turn, i, peak)
            if 0 <= turn - 1 < held:
                sums = expo_step(turn - 1, i, sums)
            if 0 <= turn - 2 < held:
                total = query_step(turn - 2, i, total)
        if turn < held:
            peaks[turn] = jnp.max(peak, axis=1, keepdims=True)
            wide_peaks[turn] = jnp.broadcast_to(peaks[turn], (q, LANES))
        if 0 <= turn - 1 < held:
            slope_x, slope_y, level = columns[turn - 1] = softmax_terms(turn - 1, *sums)
            step = jnp.broadcast_to(slope_y, (q, LANES))
            lines_of[turn - 1] = (level + slope_x * lane_x + step * lane_y, step * row_step)
            rest = [to_row(column) for column in (peaks[turn - 1],) + columns[turn - 1]]
            stats[turn - 1, me_t] = jnp.concatenate(rest + rest, axis=0)
            for d, device in track_peers:
                copy = pltpu.make_async_remote_copy(
                    src_ref=stats.at[turn - 1, me_t],
                    dst_ref=stats.at[turn - 1, me_t],
                    send_sem=stat_send.at[turn - 1, d],
                    recv_sem=stat_recv.at[turn - 1, d],
                    device_id=device,
                    device_id_type=MESH,
                )
                copy.start()
                stat_copies.append(copy)
    sends += stat_copies

    term[...] = total.reshape(n_frame, rows, channels)
    term_copies = []
    for d, device in frame_peers:
        term_copies.append(
            pltpu.make_async_remote_copy(
                src_ref=term.at[lax.rem(me_f + d, n_frame)],
                dst_ref=term_in.at[d],
                send_sem=term_send.at[d],
                recv_sem=term_recv.at[d],
                device_id=device,
                device_id_type=MESH,
            )
        )
        term_copies[-1].start()
    sends += term_copies

    for copy in feat_copies:
        copy.wait_recv()
    tracks = n_track * q
    everyone = feats[...].reshape(tracks, channels)
    scaled = everyone * jnp.bfloat16(SCORE_SCALE)
    size = max(FEAT_W, min(block, 131072 // tracks // FEAT_W * FEAT_W))
    lines = size // FEAT_W
    tiles = channels // LANES
    column_x = lax.broadcasted_iota(jnp.int32, (FEAT_W, 1), 0).astype(jnp.float32)

    for t in range(held):
        for copy in stat_copies[t * (n_track - 1) : (t + 1) * (n_track - 1)]:
            copy.wait_recv()
        levels = jnp.concatenate([stats[t, k] for k in range(n_track)], axis=1)
        peak, slope_x, slope_y, level = [levels[j : j + 1] for j in range(4)]
        slope_x = slope_x * column_x

        def frame_part(i, carry):
            start = me_t * block + i * size
            first_line = me_t * (block // FEAT_W) + i * lines
            s = dot(fr[t, pl.ds(pl.multiple_of(start, FEAT_W), size), :], scaled, ((1,), (1,)))
            e = jnp.exp(s - peak)
            at = [slope_x + (level + slope_y * (first_line + l).astype(jnp.float32)) for l in range(lines)]
            grad = (e * jnp.concatenate(at, axis=0)).astype(jnp.bfloat16)
            result = dot(grad, everyone, ((1,), (0,)))
            for c in range(tiles):
                place = pl.ds(i * (size * tiles * held) + c * held + t, size, stride=tiles * held)
                out_ref[place, :] = result[:, c * LANES : (c + 1) * LANES]
            return carry

        lax.fori_loop(0, block // size, frame_part, 0, unroll=True)

    mine = term[me_f]
    for d, copy in enumerate(term_copies, 1):
        copy.wait_recv()
        mine += term_in[d]
    query_out_ref[...] = mine
    for copy in sends:
        copy.wait_send()


def on_device(n_track, n_frame, frames, query_frame, query_pixel, cotangent):
    held, pixels, channels = frames.shape
    q = query_frame.shape[0]
    rows = q // n_frame
    block = pixels // n_track
    tiles = channels // LANES
    wide = 4 * LANES
    index = (query_frame * pixels + query_pixel).astype(jnp.float32).reshape(1, q)
    vmem = pl.BlockSpec(memory_space=pltpu.VMEM)
    dma = pltpu.SemaphoreType.DMA
    frame_grad, query_grad = pl.pallas_call(
        functools.partial(kernel, n_track, n_frame),
        out_shape=(
            jax.ShapeDtypeStruct((block * tiles * held, LANES), jnp.float32),
            jax.ShapeDtypeStruct((rows, channels), jnp.float32),
        ),
        in_specs=[pl.BlockSpec(memory_space=pltpu.HBM), vmem, vmem],
        out_specs=(vmem, vmem),
        scratch_shapes=[
            pltpu.VMEM((held, pixels, channels), jnp.bfloat16),
            pltpu.VMEM((held, pixels // wide, q, wide), jnp.float32),
            pltpu.VMEM((n_frame, rows, channels), jnp.bfloat16),
            pltpu.VMEM((n_frame, n_frame, rows, channels), jnp.bfloat16),
            pltpu.VMEM((n_track, n_frame, rows, channels), jnp.bfloat16),
            pltpu.VMEM((held, n_track, 8, q), jnp.float32),
            pltpu.VMEM((n_frame, rows, channels), jnp.float32),
            pltpu.VMEM((n_frame, rows, channels), jnp.float32),
            dma((held, 4)),
            dma((n_frame,)),
            dma((n_frame,)),
            dma((n_track,)),
            dma((n_track,)),
            dma((held, n_track)),
            dma((held, n_track)),
            dma((n_frame,)),
            dma((n_frame,)),
        ],
        compiler_params=pltpu.CompilerParams(
            collective_id=0, has_side_effects=True, vmem_limit_bytes=48 * 2**20
        ),
        name="matching_grad",
    )(frames, index, cotangent)
    frame_grad = frame_grad.reshape(block, tiles, held, LANES).transpose(0, 2, 1, 3)
    return (frame_grad.reshape(block, held, channels), query_grad)


def solution(mesh):
    return jax.shard_map(
        functools.partial(on_device, mesh.shape["track"], mesh.shape["frame"]),
        mesh=mesh,
        in_specs=(
            P(("groups", "frame"), None, None),
            P(("groups", "track")),
            P(("groups", "track")),
            P(None, ("groups", "frame"), "track"),
        ),
        out_specs=(P("track", ("groups", "frame"), None), P(("groups", "track", "frame"), None)),
        check_vma=False,
    )
```

```python
import functools

import jax
import jax.numpy as jnp
from jax import lax
from jax.experimental import pallas as pl
from jax.experimental.pallas import tpu as pltpu
from jax.sharding import PartitionSpec as P

C = 256
FEAT_H = 64
FEAT_W = 64
LANES = 128
MESH = pl.DeviceIdType.MESH
SCORE_SCALE = C ** (-0.5)
STEP_X = 2.0 / (FEAT_W - 1)
STEP_Y = 2.0 / (FEAT_H - 1)


def dot(a, b, dims):
    return lax.dot_general(a, b, (dims, ((), ())), preferred_element_type=jnp.float32)


def kernel(
    n_track,
    n_frame,
    frames_hbm,
    index_ref,
    cot_ref,
    out_ref,
    query_out_ref,
    fr,
    scores,
    picked,
    picked_in,
    feats,
    stats,
    term,
    term_in,
    load_sem,
    pick_send,
    pick_recv,
    feat_send,
    feat_recv,
    stat_send,
    stat_recv,
    term_send,
    term_recv,
):
    held, pixels, channels = fr.shape
    q = index_ref.shape[1]
    rows = q // n_frame
    block = pixels // n_track
    me_t = lax.axis_index("track")
    me_f = lax.axis_index("frame")

    def peers(name, me, n):
        return [(d, {name: lax.rem(me + d, n)}) for d in range(1, n)]

    track_peers = peers("track", me_t, n_track)
    frame_peers = peers("frame", me_f, n_frame)

    barrier = pltpu.get_barrier_semaphore()
    for _, device in track_peers + frame_peers:
        pl.semaphore_signal(barrier, inc=1, device_id=device, device_id_type=MESH)

    parts = load_sem.shape[1]
    piece = pixels // parts
    loads = []
    for t in range(held):
        for i in range(parts):
            where = pl.ds(i * piece, piece)
            load = pltpu.make_async_copy(frames_hbm.at[t, where], fr.at[t, where], load_sem.at[t, i])
            load.start()
            loads.append((t, i, load))

    eye = lax.broadcasted_iota(jnp.int32, (q, q), 0) == lax.broadcasted_iota(jnp.int32, (q, q), 1)

    def to_column(row):
        return jnp.sum(jnp.where(eye, row, jnp.zeros_like(row)), axis=1, keepdims=True)

    def to_row(column):
        return jnp.sum(jnp.where(eye, column, jnp.zeros_like(column)), axis=0, keepdims=True)

    index = to_column(index_ref[...]).astype(jnp.int32) - me_f * (held * pixels)
    lane = lax.broadcasted_iota(jnp.int32, (q, piece), 1)
    total = jnp.zeros((q, channels), jnp.float32)
    for t, i, load in loads:
        load.wait()
        hot = jnp.where(lane == index - (t * pixels + i * piece), 1.0, 0.0).astype(jnp.bfloat16)
        total += dot(hot, fr[t, i * piece : (i + 1) * piece, :], ((1,), (0,)))
    picked[...] = total.astype(jnp.bfloat16).reshape(n_frame, rows, channels)

    pl.semaphore_wait(barrier, n_track + n_frame - 2)

    halves = pick_send.shape[0]
    part = n_frame // halves
    sends, feat_copies = [], []
    picks = []
    for g in range(halves):
        picks.append([])
        for d, device in frame_peers:
            copy = pltpu.make_async_remote_copy(
                src_ref=picked.at[pl.ds(g * part, part)],
                dst_ref=picked_in.at[d, pl.ds(g * part, part)],
                send_sem=pick_send.at[g, d],
                recv_sem=pick_recv.at[g, d],
                device_id=device,
                device_id_type=MESH,
            )
            copy.start()
            picks[g].append(copy)
        sends += picks[g]

    def features(g):
        where = pl.ds(g * part, part)
        mine = picked[where].astype(jnp.float32)
        for d, copy in enumerate(picks[g], 1):
            copy.wait_recv()
            mine += picked_in[d, where].astype(jnp.float32)
        mine = mine.astype(jnp.bfloat16)
        feats[me_t, where] = mine
        for d, device in track_peers:
            copy = pltpu.make_async_remote_copy(
                src_ref=feats.at[me_t, where],
                dst_ref=feats.at[me_t, where],
                send_sem=feat_send.at[g, d],
                recv_sem=feat_recv.at[g, d],
                device_id=device,
                device_id_type=MESH,
            )
            copy.start()
            feat_copies.append(copy)
        return mine.reshape(part * rows, channels) * jnp.bfloat16(SCORE_SCALE)

    wide = scores.shape[3]
    cols = wide // LANES
    chunks = pixels // wide
    lane = lax.broadcasted_iota(jnp.int32, (q, LANES), 1)
    lane_x = (lane % FEAT_W).astype(jnp.float32)
    lane_y = (lane // FEAT_W).astype(jnp.float32)
    row_step = LANES // FEAT_W

    def split(x):
        return [x[:, c * LANES : (c + 1) * LANES] for c in range(cols)]

    def chunk_of(t, i):
        return fr[t, pl.ds(pl.multiple_of(i * wide, wide), wide), :]

    def scores_step(g, own, t, i, peak):
        s = dot(own, chunk_of(t, i), ((1,), (1,)))
        scores[t, i, g * half : (g + 1) * half, :] = s
        return functools.reduce(jnp.maximum, split(s), peak)

    def expo_step(g, wide_peak, t, i, carry):
        zero, first = carry
        e = [jnp.exp(x - wide_peak) for x in split(scores[t, i, g * half : (g + 1) * half, :])]
        scores[t, i, g * half : (g + 1) * half, :] = jnp.concatenate(e, axis=1)
        tail = e[-1]
        moment = tail
        for x in e[-2:0:-1]:
            tail = tail + x
            moment = moment + tail
        tail = tail + e[0]
        return zero + tail, first + (moment + tail * float(i * cols))

    def query_step(t, i, total):
        base, step = lines_of[t]
        grad = [
            (part * (base + step * float(i * cols + c))).astype(jnp.bfloat16)
            for c, part in enumerate(split(scores[t, i]))
        ]
        return total + dot(jnp.concatenate(grad, axis=1), chunk_of(t, i), ((1,), (0,)))

    def softmax_terms(t, zero, first):
        mass = jnp.sum(zero, axis=1, keepdims=True)
        mean_x = jnp.sum(zero * lane_x, axis=1, keepdims=True) / mass
        mean_y = jnp.sum(zero * lane_y + first * row_step, axis=1, keepdims=True) / mass
        grad_x = to_column(cot_ref[0, t : t + 1, :])
        grad_y = to_column(cot_ref[1, t : t + 1, :])
        scale = SCORE_SCALE / mass
        slope_x = grad_x * STEP_X * scale
        slope_y = grad_y * STEP_Y * scale
        return slope_x, slope_y, -(slope_x * mean_x + slope_y * mean_y)

    half = q // halves
    peaks, sums, lines_of, stat_copies = {}, {}, {}, []
    empty = jnp.zeros((half, LANES), jnp.float32)
    for g in range(halves):
        own = features(g)
        for turn in range(held + 1):
            peak = jnp.full((half, LANES), -jnp.inf, jnp.float32)
            carry = (empty, empty)
            if turn > 0:
                wide_peak = jnp.broadcast_to(peaks[g, turn - 1], (half, LANES))
            for i in range(chunks):
                if turn < held:
                    peak = scores_step(g, own, turn, i, peak)
                if turn > 0:
                    carry = expo_step(g, wide_peak, turn - 1, i, carry)
            if turn < held:
                peaks[g, turn] = jnp.max(peak, axis=1, keepdims=True)
            if turn > 0:
                sums[g, turn - 1] = carry
    for t in range(held):
        zero, first = [jnp.concatenate([sums[g, t][j] for g in range(halves)], axis=0) for j in range(2)]
        peak = jnp.concatenate([peaks[g, t] for g in range(halves)], axis=0)
        slope_x, slope_y, level = softmax_terms(t, zero, first)
        step = jnp.broadcast_to(slope_y, (q, LANES))
        lines_of[t] = (level + slope_x * lane_x + step * lane_y, step * row_step)
        rest = [to_row(column) for column in (peak, slope_x, slope_y, level)]
        stats[t, me_t] = jnp.concatenate(rest + rest, axis=0)
        for d, device in track_peers:
            copy = pltpu.make_async_remote_copy(
                src_ref=stats.at[t, me_t],
                dst_ref=stats.at[t, me_t],
                send_sem=stat_send.at[t, d],
                recv_sem=stat_recv.at[t, d],
                device_id=device,
                device_id_type=MESH,
            )
            copy.start()
            stat_copies.append(copy)
    sends += feat_copies
    total = jnp.zeros((q, channels), jnp.float32)
    for t in range(held):
        for i in range(chunks):
            total = query_step(t, i, total)
    sends += stat_copies

    term[...] = total.reshape(n_frame, rows, channels)
    term_copies = []
    for d, device in frame_peers:
        term_copies.append(
            pltpu.make_async_remote_copy(
                src_ref=term.at[lax.rem(me_f + d, n_frame)],
                dst_ref=term_in.at[d],
                send_sem=term_send.at[d],
                recv_sem=term_recv.at[d],
                device_id=device,
                device_id_type=MESH,
            )
        )
        term_copies[-1].start()
    sends += term_copies

    for copy in feat_copies:
        copy.wait_recv()
    tracks = n_track * q
    everyone = feats[...].reshape(tracks, channels)
    scaled = everyone * jnp.bfloat16(SCORE_SCALE)
    size = max(FEAT_W, min(block, 131072 // tracks // FEAT_W * FEAT_W))
    lines = size // FEAT_W
    tiles = channels // LANES
    column_x = lax.broadcasted_iota(jnp.int32, (FEAT_W, 1), 0).astype(jnp.float32)

    for t in range(held):
        for copy in stat_copies[t * (n_track - 1) : (t + 1) * (n_track - 1)]:
            copy.wait_recv()
        levels = jnp.concatenate([stats[t, k] for k in range(n_track)], axis=1)
        peak, slope_x, slope_y, level = [levels[j : j + 1] for j in range(4)]
        slope_x = slope_x * column_x

        def frame_part(i, carry):
            start = me_t * block + i * size
            first_line = me_t * (block // FEAT_W) + i * lines
            s = dot(fr[t, pl.ds(pl.multiple_of(start, FEAT_W), size), :], scaled, ((1,), (1,)))
            e = jnp.exp(s - peak)
            at = [slope_x + (level + slope_y * (first_line + l).astype(jnp.float32)) for l in range(lines)]
            grad = (e * jnp.concatenate(at, axis=0)).astype(jnp.bfloat16)
            result = dot(grad, everyone, ((1,), (0,)))
            for c in range(tiles):
                place = pl.ds(i * (size * tiles * held) + c * held + t, size, stride=tiles * held)
                out_ref[place, :] = result[:, c * LANES : (c + 1) * LANES]
            return carry

        lax.fori_loop(0, block // size, frame_part, 0, unroll=True)

    mine = term[me_f]
    for d, copy in enumerate(term_copies, 1):
        copy.wait_recv()
        mine += term_in[d]
    query_out_ref[...] = mine
    for copy in sends:
        copy.wait_send()


def on_device(n_track, n_frame, frames, query_frame, query_pixel, cotangent):
    held, pixels, channels = frames.shape
    q = query_frame.shape[0]
    rows = q // n_frame
    block = pixels // n_track
    tiles = channels // LANES
    wide = 4 * LANES
    halves = 2 if n_frame % 2 == 0 and (q // 2) % 16 == 0 else 1
    index = (query_frame * pixels + query_pixel).astype(jnp.float32).reshape(1, q)
    vmem = pl.BlockSpec(memory_space=pltpu.VMEM)
    dma = pltpu.SemaphoreType.DMA
    frame_grad, query_grad = pl.pallas_call(
        functools.partial(kernel, n_track, n_frame),
        out_shape=(
            jax.ShapeDtypeStruct((block * tiles * held, LANES), jnp.float32),
            jax.ShapeDtypeStruct((rows, channels), jnp.float32),
        ),
        in_specs=[pl.BlockSpec(memory_space=pltpu.HBM), vmem, vmem],
        out_specs=(vmem, vmem),
        scratch_shapes=[
            pltpu.VMEM((held, pixels, channels), jnp.bfloat16),
            pltpu.VMEM((held, pixels // wide, q, wide), jnp.float32),
            pltpu.VMEM((n_frame, rows, channels), jnp.bfloat16),
            pltpu.VMEM((n_frame, n_frame, rows, channels), jnp.bfloat16),
            pltpu.VMEM((n_track, n_frame, rows, channels), jnp.bfloat16),
            pltpu.VMEM((held, n_track, 8, q), jnp.float32),
            pltpu.VMEM((n_frame, rows, channels), jnp.float32),
            pltpu.VMEM((n_frame, rows, channels), jnp.float32),
            dma((held, 4)),
            dma((halves, n_frame)),
            dma((halves, n_frame)),
            dma((halves, n_track)),
            dma((halves, n_track)),
            dma((held, n_track)),
            dma((held, n_track)),
            dma((n_frame,)),
            dma((n_frame,)),
        ],
        compiler_params=pltpu.CompilerParams(
            collective_id=0, has_side_effects=True, vmem_limit_bytes=48 * 2**20
        ),
        name="matching_grad",
    )(frames, index, cotangent)
    frame_grad = frame_grad.reshape(block, tiles, held, LANES).transpose(0, 2, 1, 3)
    return (frame_grad.reshape(block, held, channels), query_grad)


def solution(mesh):
    return jax.shard_map(
        functools.partial(on_device, mesh.shape["track"], mesh.shape["frame"]),
        mesh=mesh,
        in_specs=(
            P(("groups", "frame"), None, None),
            P(("groups", "track")),
            P(("groups", "track")),
            P(None, ("groups", "frame"), "track"),
        ),
        out_specs=(P("track", ("groups", "frame"), None), P(("groups", "track", "frame"), None)),
        check_vma=False,
    )
```

```python
import functools

import jax
import jax.numpy as jnp
from jax import lax
from jax.experimental import pallas as pl
from jax.experimental.pallas import tpu as pltpu
from jax.sharding import PartitionSpec as P

C = 256
FEAT_H = 64
FEAT_W = 64
LANES = 128
MESH = pl.DeviceIdType.MESH
SCORE_SCALE = C ** (-0.5)
STEP_X = 2.0 / (FEAT_W - 1)
STEP_Y = 2.0 / (FEAT_H - 1)


def dot(a, b, dims):
    return lax.dot_general(a, b, (dims, ((), ())), preferred_element_type=jnp.float32)


def kernel(
    n_track,
    n_frame,
    frames_hbm,
    index_ref,
    cot_ref,
    out_ref,
    query_out_ref,
    fr,
    scores,
    picked,
    picked_in,
    feats,
    stats,
    term,
    term_in,
    load_sem,
    pick_send,
    pick_recv,
    feat_send,
    feat_recv,
    stat_send,
    stat_recv,
    term_send,
    term_recv,
):
    held, pixels, channels = fr.shape
    q = index_ref.shape[1]
    rows = q // n_frame
    block = pixels // n_track
    me_t = lax.axis_index("track")
    me_f = lax.axis_index("frame")

    def peers(name, me, n):
        return [(d, {name: lax.rem(me + d, n)}) for d in range(1, n)]

    track_peers = peers("track", me_t, n_track)
    frame_peers = peers("frame", me_f, n_frame)

    barrier = pltpu.get_barrier_semaphore()
    for _, device in track_peers + frame_peers:
        pl.semaphore_signal(barrier, inc=1, device_id=device, device_id_type=MESH)

    parts = load_sem.shape[1]
    piece = pixels // parts
    loads = []
    for t in range(held):
        for i in range(parts):
            where = pl.ds(i * piece, piece)
            load = pltpu.make_async_copy(frames_hbm.at[t, where], fr.at[t, where], load_sem.at[t, i])
            load.start()
            loads.append((t, i, load))

    eye = lax.broadcasted_iota(jnp.int32, (q, q), 0) == lax.broadcasted_iota(jnp.int32, (q, q), 1)

    def to_column(row):
        return jnp.sum(jnp.where(eye, row, jnp.zeros_like(row)), axis=1, keepdims=True)

    def to_row(column):
        return jnp.sum(jnp.where(eye, column, jnp.zeros_like(column)), axis=0, keepdims=True)

    index = to_column(index_ref[...]).astype(jnp.int32) - me_f * (held * pixels)
    lane = lax.broadcasted_iota(jnp.int32, (q, piece), 1)
    total = jnp.zeros((q, channels), jnp.float32)
    for t, i, load in loads:
        load.wait()
        hot = jnp.where(lane == index - (t * pixels + i * piece), 1.0, 0.0).astype(jnp.bfloat16)
        total += dot(hot, fr[t, i * piece : (i + 1) * piece, :], ((1,), (0,)))
    picked[...] = total.astype(jnp.bfloat16).reshape(n_frame, rows, channels)

    pl.semaphore_wait(barrier, n_track + n_frame - 2)

    copies = []
    for d, device in frame_peers:
        copies.append(
            pltpu.make_async_remote_copy(
                src_ref=picked,
                dst_ref=picked_in.at[d],
                send_sem=pick_send.at[d],
                recv_sem=pick_recv.at[d],
                device_id=device,
                device_id_type=MESH,
            )
        )
        copies[-1].start()
    mine = picked[...].astype(jnp.float32)
    for d, copy in enumerate(copies, 1):
        copy.wait_recv()
        mine += picked_in[d].astype(jnp.float32)
    feats[me_t] = mine.astype(jnp.bfloat16)
    sends = copies
    feat_copies = []
    for d, device in track_peers:
        feat_copies.append(
            pltpu.make_async_remote_copy(
                src_ref=feats.at[me_t],
                dst_ref=feats.at[me_t],
                send_sem=feat_send.at[d],
                recv_sem=feat_recv.at[d],
                device_id=device,
                device_id_type=MESH,
            )
        )
        feat_copies[-1].start()
    sends += feat_copies

    own = feats[me_t].reshape(q, channels) * jnp.bfloat16(SCORE_SCALE)
    wide = scores.shape[3]
    cols = wide // LANES
    chunks = pixels // wide
    lane = lax.broadcasted_iota(jnp.int32, (q, LANES), 1)
    lane_x = (lane % FEAT_W).astype(jnp.float32)
    lane_y = (lane // FEAT_W).astype(jnp.float32)
    row_step = LANES // FEAT_W

    def split(x):
        return [x[:, c * LANES : (c + 1) * LANES] for c in range(cols)]

    def chunk_of(t, i):
        return fr[t, pl.ds(pl.multiple_of(i * wide, wide), wide), :]

    def scores_step(t, i, peak):
        s = dot(own, chunk_of(t, i), ((1,), (1,)))
        scores[t, i] = s
        return functools.reduce(jnp.maximum, split(s), peak)

    def expo_step(t, i, carry):
        zero, first = carry
        e = [jnp.exp(part - wide_peaks[t]) for part in split(scores[t, i])]
        scores[t, i] = jnp.concatenate(e, axis=1)
        tail = e[-1]
        moment = tail
        for part in e[-2:0:-1]:
            tail = tail + part
            moment = moment + tail
        tail = tail + e[0]
        return zero + tail, first + (moment + tail * float(i * cols))

    def query_step(t, i, total):
        base, step = lines_of[t]
        grad = [
            (part * (base + step * float(i * cols + c))).astype(jnp.bfloat16)
            for c, part in enumerate(split(scores[t, i]))
        ]
        return total + dot(jnp.concatenate(grad, axis=1), chunk_of(t, i), ((1,), (0,)))

    def softmax_terms(t, zero, first):
        mass = jnp.sum(zero, axis=1, keepdims=True)
        mean_x = jnp.sum(zero * lane_x, axis=1, keepdims=True) / mass
        mean_y = jnp.sum(zero * lane_y + first * row_step, axis=1, keepdims=True) / mass
        grad_x = to_column(cot_ref[0, t : t + 1, :])
        grad_y = to_column(cot_ref[1, t : t + 1, :])
        scale = SCORE_SCALE / mass
        slope_x = grad_x * STEP_X * scale
        slope_y = grad_y * STEP_Y * scale
        return slope_x, slope_y, -(slope_x * mean_x + slope_y * mean_y)

    peaks, wide_peaks, columns, lines_of, stat_copies = {}, {}, {}, {}, []
    total = jnp.zeros((q, channels), jnp.float32)
    empty = jnp.zeros((q, LANES), jnp.float32)
    for turn in range(held + 2):
        peak = jnp.full((q, LANES), -jnp.inf, jnp.float32)
        sums = (empty, empty)
        for i in range(chunks):
            if turn < held:
                peak = scores_step(turn, i, peak)
            if 0 <= turn - 1 < held:
                sums = expo_step(turn - 1, i, sums)
            if 0 <= turn - 2 < held:
                total = query_step(turn - 2, i, total)
        if turn < held:
            peaks[turn] = jnp.max(peak, axis=1, keepdims=True)
            wide_peaks[turn] = jnp.broadcast_to(peaks[turn], (q, LANES))
        if 0 <= turn - 1 < held:
            slope_x, slope_y, level = columns[turn - 1] = softmax_terms(turn - 1, *sums)
            step = jnp.broadcast_to(slope_y, (q, LANES))
            lines_of[turn - 1] = (level + slope_x * lane_x + step * lane_y, step * row_step)
            rest = [to_row(column) for column in (peaks[turn - 1],) + columns[turn - 1]]
            stats[turn - 1, me_t] = jnp.concatenate(rest + rest, axis=0)
            for d, device in track_peers:
                copy = pltpu.make_async_remote_copy(
                    src_ref=stats.at[turn - 1, me_t],
                    dst_ref=stats.at[turn - 1, me_t],
                    send_sem=stat_send.at[turn - 1, d],
                    recv_sem=stat_recv.at[turn - 1, d],
                    device_id=device,
                    device_id_type=MESH,
                )
                copy.start()
                stat_copies.append(copy)
    sends += stat_copies

    term[...] = total.reshape(n_frame, rows, channels)
    term_copies = []
    for d, device in frame_peers:
        term_copies.append(
            pltpu.make_async_remote_copy(
                src_ref=term.at[lax.rem(me_f + d, n_frame)],
                dst_ref=term_in.at[d],
                send_sem=term_send.at[d],
                recv_sem=term_recv.at[d],
                device_id=device,
                device_id_type=MESH,
            )
        )
        term_copies[-1].start()
    sends += term_copies

    for copy in feat_copies:
        copy.wait_recv()
    tracks = n_track * q
    everyone = feats[...].reshape(tracks, channels)
    scaled = everyone * jnp.bfloat16(SCORE_SCALE)
    size = max(FEAT_W, min(block, 131072 // tracks // FEAT_W * FEAT_W))
    lines = size // FEAT_W
    tiles = channels // LANES
    column_x = lax.broadcasted_iota(jnp.int32, (FEAT_W, 1), 0).astype(jnp.float32)

    for t in range(held):
        for copy in stat_copies[t * (n_track - 1) : (t + 1) * (n_track - 1)]:
            copy.wait_recv()
        levels = jnp.concatenate([stats[t, k] for k in range(n_track)], axis=1)
        peak, slope_x, slope_y, level = [levels[j : j + 1] for j in range(4)]
        slope_x = slope_x * column_x

        def frame_part(i, carry):
            start = me_t * block + i * size
            first_line = me_t * (block // FEAT_W) + i * lines
            s = dot(fr[t, pl.ds(pl.multiple_of(start, FEAT_W), size), :], scaled, ((1,), (1,)))
            e = jnp.exp(s - peak)
            at = [slope_x + (level + slope_y * (first_line + l).astype(jnp.float32)) for l in range(lines)]
            grad = (e * jnp.concatenate(at, axis=0)).astype(jnp.bfloat16)
            result = dot(grad, everyone, ((1,), (0,)))
            for c in range(tiles):
                place = pl.ds(i * (size * tiles * held) + c * held + t, size, stride=tiles * held)
                out_ref[place, :] = result[:, c * LANES : (c + 1) * LANES]
            return carry

        lax.fori_loop(0, block // size, frame_part, 0, unroll=True)

    mine = term[me_f]
    for d, copy in enumerate(term_copies, 1):
        copy.wait_recv()
        mine += term_in[d]
    query_out_ref[...] = mine
    for copy in sends:
        copy.wait_send()


def on_device(n_track, n_frame, frames, query_frame, query_pixel, cotangent):
    held, pixels, channels = frames.shape
    q = query_frame.shape[0]
    rows = q // n_frame
    block = pixels // n_track
    tiles = channels // LANES
    wide = 8 * LANES
    index = (query_frame * pixels + query_pixel).astype(jnp.float32).reshape(1, q)
    vmem = pl.BlockSpec(memory_space=pltpu.VMEM)
    dma = pltpu.SemaphoreType.DMA
    frame_grad, query_grad = pl.pallas_call(
        functools.partial(kernel, n_track, n_frame),
        out_shape=(
            jax.ShapeDtypeStruct((block * tiles * held, LANES), jnp.float32),
            jax.ShapeDtypeStruct((rows, channels), jnp.float32),
        ),
        in_specs=[pl.BlockSpec(memory_space=pltpu.HBM), vmem, vmem],
        out_specs=(vmem, vmem),
        scratch_shapes=[
            pltpu.VMEM((held, pixels, channels), jnp.bfloat16),
            pltpu.VMEM((held, pixels // wide, q, wide), jnp.float32),
            pltpu.VMEM((n_frame, rows, channels), jnp.bfloat16),
            pltpu.VMEM((n_frame, n_frame, rows, channels), jnp.bfloat16),
            pltpu.VMEM((n_track, n_frame, rows, channels), jnp.bfloat16),
            pltpu.VMEM((held, n_track, 8, q), jnp.float32),
            pltpu.VMEM((n_frame, rows, channels), jnp.float32),
            pltpu.VMEM((n_frame, rows, channels), jnp.float32),
            dma((held, 4)),
            dma((n_frame,)),
            dma((n_frame,)),
            dma((n_track,)),
            dma((n_track,)),
            dma((held, n_track)),
            dma((held, n_track)),
            dma((n_frame,)),
            dma((n_frame,)),
        ],
        compiler_params=pltpu.CompilerParams(
            collective_id=0, has_side_effects=True, vmem_limit_bytes=48 * 2**20
        ),
        name="matching_grad",
    )(frames, index, cotangent)
    frame_grad = frame_grad.reshape(block, tiles, held, LANES).transpose(0, 2, 1, 3)
    return (frame_grad.reshape(block, held, channels), query_grad)


def solution(mesh):
    return jax.shard_map(
        functools.partial(on_device, mesh.shape["track"], mesh.shape["frame"]),
        mesh=mesh,
        in_specs=(
            P(("groups", "frame"), None, None),
            P(("groups", "track")),
            P(("groups", "track")),
            P(None, ("groups", "frame"), "track"),
        ),
        out_specs=(P("track", ("groups", "frame"), None), P(("groups", "track", "frame"), None)),
        check_vma=False,
    )
```
